256 devices in a mesh: tok: 64 (over z, x, core), proto: 4 (over y).
Axes of the slice: x: 4, y: 4, z: 8, core: 2. Of those that a mesh axis runs over, the one named last changes fastest.
Arguments:
- teacher_seq: bfloat16 [16384, 256], P('tok')
- student_seq: bfloat16 [16384, 256], P('tok')
- prototypes: bfloat16 [256, 65536], P(None, 'proto')
- positions: int32 [8192], P('tok'), may hold values from 0 to 255
- languages: int32 [8192], P('tok'), may hold values from 0 to 99
Outputs:
- loss: float32 [], replicated
- grad_student_seq: float32 [16384, 256], P('tok')
- grad_prototypes: float32 [256, 65536], P('tok', 'proto')
The draws below stay inside these ranges and needn't reach their ends.
Inputs may be any that keep to these rules, and one draw needn't show every extreme that they name: Token i names a position within the block of 256 positions of rows (i // 128) * 256 onward; positions may repeat.
All inputs are finite; a program needn't handle non-finite values.
Results may differ from the reference program's by a relative error of at most 0.0025.
Values may be sent and summed in bfloat16 or wider, within the bound.
No kernel may reach another device: no remote copies, remote signals or barrier semaphores. Data moves between devices by JAX's collectives and lax.ppermute only.
A program may use at most 128 MiB of HBM per device.

```python
import math
from functools import partial
import jax
import jax.numpy as jnp
from jax import lax

F = 256
K = 65536
LANGS = 100
TOK_DEV = 128
ITERS = 3
SEQ_DEV = 256
TOKENS = 8192
SEQ = 16384


def shared_directions(key):
    return jax.random.normal(jax.random.fold_in(key, 7), (4, F), jnp.float32) / math.sqrt(F)


def block_layout(key):
    block_total = SEQ // SEQ_DEV
    chosen = jax.random.randint(jax.random.fold_in(key, 8), (block_total,), 0, 4, dtype=jnp.int32)
    strength = jax.random.uniform(jax.random.fold_in(key, 9), (block_total,), jnp.float32, 0.0, 1.0)
    block_of = jnp.arange(SEQ, dtype=jnp.int32) // SEQ_DEV
    return (chosen[block_of], strength[block_of])


def feature_rows(key, along, strength, lowest, highest, span):
    noise_key, scale_key = jax.random.split(key)
    noise_values = jax.random.normal(noise_key, (SEQ, F), jnp.float32)
    mixing = lowest * jnp.exp(strength * math.log(highest / lowest))[:, None]
    scales = jnp.exp(jax.random.uniform(scale_key, (SEQ, 1), jnp.float32, 0.0, math.log(span)))
    return ((noise_values / math.sqrt(F) + mixing * along) * scales).astype(jnp.bfloat16)


def draw_teacher_seq(key, part):
    directions = shared_directions(key)
    chosen, strength = block_layout(key)
    along = directions[chosen]
    key = jax.random.fold_in(key, 1)
    return feature_rows(key, along, strength, 0.6, 2.4, 10.0)


def draw_student_seq(key, part):
    directions = shared_directions(key)
    chosen, strength = block_layout(key)
    along = directions[chosen]
    key = jax.random.fold_in(key, 2)
    return feature_rows(key, along, strength, 0.3, 1.2, 10.0)


def draw_prototypes(key, part):
    directions = shared_directions(key)
    key = jax.random.fold_in(key, 3)
    noise_key, coeff_key, scale_key = jax.random.split(key, 3)
    column_frac = jnp.arange(K, dtype=jnp.float32) / (K - 1)
    noise_values = jax.random.normal(noise_key, (F, K), jnp.float32)
    coeff = 0.5 * jax.random.normal(coeff_key, (4, K), jnp.float32)
    rising = 0.5 + 1.5 * column_frac
    scales = jnp.exp(jax.random.uniform(scale_key, (1, K), jnp.float32, math.log(0.1), 0.0))
    structured = jnp.zeros((F, K), jnp.float32)
    for direction_index in range(4):
        structured = structured + directions[direction_index][:, None] * coeff[direction_index][None, :]
    return ((noise_values / math.sqrt(F) + structured * rising[None, :]) * scales).astype(jnp.bfloat16)


def draw_languages(key, part):
    key = jax.random.fold_in(key, 11)
    index_all = jnp.arange(TOKENS, dtype=jnp.int32)
    device_index = index_all // TOK_DEV
    device_count = TOKENS // TOK_DEV
    quarter = LANGS // 4
    upper = quarter + (LANGS - quarter) * device_index // max(device_count - 1, 1)
    raw_bits = jax.random.randint(key, (TOKENS,), 0, 1 << 20, dtype=jnp.int32)
    drawn = raw_bits % upper
    within = index_all % TOK_DEV
    drawn = jnp.where(within == 0, upper - 1, jnp.where(within == 1, 0, drawn))
    return drawn.astype(jnp.int32)


def touch_ends(values, rng, low, high):
    longest = values.shape.index(max(values.shape))
    spots = []
    for shift in (0, 1):
        where = [jax.random.randint(jax.random.fold_in(rng, axis), (), 0, length) for axis, length in enumerate(values.shape)]
        where[longest] = (where[longest] + shift) % values.shape[longest]
        spots.append(tuple(where))
    return values.at[spots[0]].set(low).at[spots[1]].set(high)


def setup_inputs(seed: int = 0) -> dict:
    key_list = jax.random.split(jax.random.key(seed), 6)
    teacher_seq = draw_teacher_seq(jax.random.fold_in(key_list[5], 71), 0)
    student_seq = draw_student_seq(jax.random.fold_in(key_list[5], 71), 0)
    prototypes = draw_prototypes(jax.random.fold_in(key_list[5], 71), 0)
    positions = touch_ends(jax.random.randint(key_list[3], (TOKENS,), 0, SEQ_DEV), jax.random.fold_in(key_list[3], 1), 0, SEQ_DEV - 1).astype(jnp.int32)
    languages = draw_languages(jax.random.fold_in(key_list[5], 71), 0)
    return dict(teacher_seq=teacher_seq, student_seq=student_seq, prototypes=prototypes, positions=positions, languages=languages)


epsilon = 1e-06
teacher_temp = 0.05
student_temp = 0.1
grad_scale = 8388608.0

def unit_rows(values):
    floats = values.astype(jnp.float32)
    inverse = lax.rsqrt(lax.optimization_barrier(jnp.sum(floats * floats, axis=1, keepdims=True)) + epsilon)
    return (floats * inverse, inverse)

def teacher_block(teacher_unit, weight_block):
    return jnp.exp(jnp.dot(teacher_unit, weight_block, preferred_element_type=jnp.float32) / teacher_temp)

def column_factor(teacher_unit, row_weight, weight_block):
    return 1.0 / lax.optimization_barrier(jnp.sum(teacher_block(teacher_unit, weight_block) * row_weight[:, None], axis=0))

def reference(teacher_seq, student_seq, prototypes, positions, languages):
    row_index = jnp.arange(TOKENS, dtype=jnp.int32) // TOK_DEV * SEQ_DEV + positions
    teacher_rows = teacher_seq[row_index]
    student_rows = student_seq[row_index]
    teacher_unit = unit_rows(teacher_rows)[0].astype(jnp.bfloat16)
    student_float, student_inv = unit_rows(student_rows)
    student_unit = student_float.astype(jnp.bfloat16)
    student_plain = student_rows.astype(jnp.float32)
    weights = prototypes.astype(jnp.float32)
    weight_inv = lax.rsqrt(lax.optimization_barrier(jnp.sum(weights * weights, axis=0)) + epsilon)
    weight_unit = (weights * weight_inv[None, :]).astype(jnp.bfloat16)
    block_width = min(K, 4096)
    block_count = K // block_width
    unit_blocks = weight_unit.reshape(F, block_count, block_width).transpose(1, 0, 2)
    plain_blocks = weights.reshape(F, block_count, block_width).transpose(1, 0, 2)
    inv_blocks = weight_inv.reshape(block_count, block_width)

    def row_factor(col_blocks):

        def accumulate(running, element):
            weight_block, col_part = element
            exps = teacher_block(teacher_unit, weight_block)
            return (running + lax.optimization_barrier(jnp.sum(exps * col_part[None, :], axis=1)), None)
        running, _ = lax.scan(accumulate, jnp.zeros((TOKENS,), jnp.float32), (unit_blocks, col_blocks))
        return 1.0 / running
    col_weight = jnp.ones((block_count, block_width), jnp.float32)
    row_weight = row_factor(col_weight)
    for sweep_index in range(ITERS):
        col_weight = lax.map(partial(column_factor, teacher_unit, row_weight), unit_blocks)
        row_weight = row_factor(col_weight)

    def gather_stats(running, element):
        weight_block, col_part = element
        target = teacher_block(teacher_unit, weight_block) * row_weight[:, None] * col_part[None, :]
        logits = jnp.dot(student_unit, weight_block, preferred_element_type=jnp.float32) / student_temp
        return ((running[0] + lax.optimization_barrier(jnp.sum(jnp.exp(logits), axis=1)), running[1] + lax.optimization_barrier(jnp.sum(target, axis=1)), running[2] + lax.optimization_barrier(jnp.sum(target * logits, axis=1))), None)
    zeros = jnp.zeros((TOKENS,), jnp.float32)
    (exp_sum, target_sum, target_dot), _ = lax.scan(gather_stats, (zeros, zeros, zeros), (unit_blocks, col_weight))
    log_total = jnp.log(exp_sum)
    cross = log_total * target_sum - target_dot
    onehot = (languages[:, None] == jnp.arange(LANGS, dtype=jnp.int32)[None, :]).astype(jnp.float32)
    counts = lax.optimization_barrier(jnp.sum(onehot, axis=0))
    present = jnp.sum((counts > 0.5).astype(jnp.float32))
    token_weight = 1.0 / (counts[languages] * present)
    loss = jnp.sum(token_weight * cross)

    def backward(running, element):
        weight_block, col_part, plain_block, inv_part = element
        target = teacher_block(teacher_unit, weight_block) * row_weight[:, None] * col_part[None, :]
        logits = jnp.dot(student_unit, weight_block, preferred_element_type=jnp.float32) / student_temp
        softmax = jnp.exp(logits - log_total[:, None])
        grad_logits = (grad_scale * token_weight[:, None] * (softmax * target_sum[:, None] - target)).astype(jnp.bfloat16)
        running = running + jnp.dot(grad_logits, weight_block.T, preferred_element_type=jnp.float32)
        grad_unit_w = jnp.dot(student_unit.T, grad_logits, preferred_element_type=jnp.float32) / student_temp
        inner = lax.optimization_barrier(jnp.sum(plain_block * grad_unit_w, axis=0))
        grad_block = inv_part[None, :] * grad_unit_w - plain_block * (inv_part ** 3)[None, :] * inner[None, :]
        return (running, grad_block)
    grad_raw, grad_blocks = lax.scan(backward, jnp.zeros((TOKENS, F), jnp.float32), (unit_blocks, col_weight, plain_blocks, inv_blocks))
    grad_prototypes = grad_blocks.transpose(1, 0, 2).reshape(F, K)
    grad_unit = grad_raw / student_temp
    along = lax.optimization_barrier(jnp.sum(student_plain * grad_unit, axis=1, keepdims=True))
    grad_rows = student_inv * grad_unit - student_plain * student_inv ** 3 * along
    grad_student_seq = jnp.zeros((SEQ, F), jnp.float32).at[row_index].add(grad_rows)
    return (loss, grad_student_seq, grad_prototypes)
```

```python
import jax
import jax.numpy as jnp
from jax import lax
from jax.experimental import pallas as pl
from jax.experimental.pallas import tpu as pltpu
from jax.sharding import Mesh, PartitionSpec as P

LANGS = 100
ITERS = 3

epsilon = 1e-06
teacher_scale = 20.0
student_scale = 10.0
grad_scale = 8388608.0

Z, X, C, Y = 8, 4, 2, 4
TOK = 128
GROUPS = X * C
ROWS = GROUPS * TOK
COLS = 2048
FEAT = 256
LANE = 128
CHUNK = 256
PEERS = X * C * Y
SHARE = ROWS // PEERS
LOSS_LANES = 128
f32 = jnp.float32
bf16 = jnp.bfloat16


def call(kernel, out_shape, scratch=(), smem_first=False, mib=16):
    def run(*args):
        in_specs = [pl.BlockSpec(memory_space=pltpu.VMEM)] * len(args)
        if smem_first:
            in_specs[0] = pl.BlockSpec(memory_space=pltpu.SMEM)
        multiple = isinstance(out_shape, (tuple, list))
        out_specs = pl.BlockSpec(memory_space=pltpu.VMEM)
        return pl.pallas_call(
            kernel,
            out_shape=out_shape,
            in_specs=in_specs,
            out_specs=[out_specs] * len(out_shape) if multiple else out_specs,
            scratch_shapes=list(scratch),
            compiler_params=pltpu.CompilerParams(vmem_limit_bytes=mib << 20),
            name=kernel.__name__,
        )(*args)

    return run


def lanes(row):
    return jnp.broadcast_to(row, (LANE, LANE)).T


def row_totals(block):
    return jnp.sum(block.T, axis=0, keepdims=True)


def blk(index):
    return pl.ds(index * LANE, LANE)


def split(values):
    high = values.astype(bf16)
    return high, (values - high.astype(f32)).astype(bf16)


def nt(left, right):
    return lax.dot_general(left, right, (((1,), (1,)), ((), ())), preferred_element_type=f32)


def tn(left, right):
    return lax.dot_general(left, right, (((0,), (0,)), ((), ())), preferred_element_type=f32)


def unit_inverse(values):
    return lax.rsqrt(jnp.sum(values * values, axis=1, keepdims=True) + epsilon)


def pick_rows(pos_ref, lang_ref, teacher_ref, student_ref, out_ref, rows_ref):
    where = lax.broadcasted_iota(jnp.int32, (FEAT, TOK), 0) == pos_ref[...]
    picker = jnp.where(where, 1.0, 0.0).astype(bf16)
    teacher = tn(picker, teacher_ref[...])
    student = tn(picker, student_ref[...])
    teacher_unit = (teacher * unit_inverse(teacher)).astype(bf16)
    student_unit = (student * unit_inverse(student)).astype(bf16)
    language = jnp.broadcast_to(lang_ref[...].astype(f32), (16, TOK)).astype(bf16)
    rows_ref[...] = student
    for peer in range(GROUPS):
        out_ref[peer, 0:TOK, 0:FEAT] = teacher_unit
        out_ref[peer, 0:TOK, FEAT : 2 * FEAT] = student_unit
        for part in range(4):
            out_ref[peer, TOK : TOK + 16, part * LANE : (part + 1) * LANE] = language


def start(recv_ref, w_ref, e_ref, unit_ref, inv_ref, student_ref, lang_ref, count_ref, msg_ref, x_ref, acc_ref, d_ref):
    for k in range(GROUPS):
        x_ref[blk(k), :] = recv_ref[k, 0:TOK, 0:FEAT]
        student_ref[blk(k), :] = recv_ref[k, 0:TOK, FEAT : 2 * FEAT]
        lang_ref[k : k + 1, :] = recv_ref[k, TOK : TOK + 16, 0:LANE].astype(f32)[0:1, :]
    hits = jnp.zeros((LANE, LANE), f32)
    number = lax.broadcasted_iota(jnp.int32, (LANE, LANE), 0).astype(f32)
    for k in range(GROUPS):
        hits = hits + jnp.where(number == lang_ref[k : k + 1, :], 1.0, 0.0)
    count_ref[...] = jnp.broadcast_to(row_totals(hits), (8, LANE))
    acc_ref[...] = jnp.zeros((ROWS, LANE), f32)

    def step(chunk, _):
        cols = pl.ds(pl.multiple_of(chunk * CHUNK, CHUNK), CHUNK)
        w = w_ref[:, cols].astype(f32)
        inv = lax.rsqrt(jnp.sum(w * w, axis=0, keepdims=True) + epsilon)
        inv_ref[:, cols] = inv
        unit = (w * inv).astype(bf16)
        unit_ref[:, cols] = unit
        d_ref[...] = jnp.dot(x_ref[...], unit, preferred_element_type=f32)
        for k in range(GROUPS):
            e = jnp.exp(d_ref[blk(k), :] * teacher_scale)
            e_ref[blk(k), cols] = e
            acc_ref[blk(k), :] += e[:, :LANE] + e[:, LANE:]
        return 0

    lax.fori_loop(0, COLS // CHUNK, step, 0)
    sums = jnp.concatenate([row_totals(acc_ref[blk(k), :]) for k in range(GROUPS)], axis=0)
    for peer in range(PEERS):
        msg_ref[peer] = sums


def peer_sum(recv_ref, low, high):
    total = recv_ref[0, low:high, :]
    for peer in range(1, recv_ref.shape[0]):
        total = total + recv_ref[peer, low:high, :]
    return total


def column_pass(recv_ref, e_ref, count_ref, msg_ref, acc_ref):
    row_weight = 1.0 / peer_sum(recv_ref, 0, GROUPS)
    for k in range(GROUPS):
        factor = lanes(row_weight[k : k + 1, :])
        for j in range(COLS // LANE):
            part = jnp.sum((e_ref[blk(k), blk(j)] * factor).reshape(LANE // 8, 8, LANE), axis=0)
            acc_ref[j] = part if k == 0 else acc_ref[j] + part
    sums = jnp.concatenate([jnp.sum(acc_ref[j], axis=0, keepdims=True) for j in range(COLS // LANE)], axis=0)
    for peer in range(Z):
        msg_ref[peer, 0:16, :] = sums
        if msg_ref.shape[1] > 16:
            msg_ref[peer, 16:24, :] = count_ref[...]


def weighted_rows(e_ref, col_weight):
    out = []
    for k in range(GROUPS):
        acc = e_ref[blk(k), blk(0)] * col_weight[0:1, :]
        for j in range(1, COLS // LANE):
            acc = acc + e_ref[blk(k), blk(j)] * col_weight[j : j + 1, :]
        out.append(row_totals(acc))
    return jnp.concatenate(out, axis=0)


def row_pass(recv_ref, e_ref, msg_ref, count_ref):
    col_weight = 1.0 / peer_sum(recv_ref, 0, 16)
    if recv_ref.shape[1] > 16:
        count_ref[...] = peer_sum(recv_ref, 16, 24)
    else:
        count_ref[...] = jnp.zeros((8, LANE), f32)
    sums = weighted_rows(e_ref, col_weight)
    for peer in range(PEERS):
        msg_ref[peer] = sums


def send_shares(msg_ref, first, second, u_ref):
    for peer in range(PEERS):
        msg_ref[peer, 0:8, :] = first
        msg_ref[peer, 8:16, :] = second
        share = pl.ds(peer * SHARE, SHARE)
        msg_ref[peer, 16 : 16 + SHARE, :] = u_ref[share, 0:LANE]
        msg_ref[peer, 16 + SHARE : 16 + 2 * SHARE, :] = u_ref[share, LANE : 2 * LANE]


def row_pass_student(recv_ref, e_ref, student_ref, unit_ref, msg_ref, acc_ref, u_ref, d_ref, high_ref, low_ref):
    col_weight = 1.0 / peer_sum(recv_ref, 0, 16)
    sums = weighted_rows(e_ref, col_weight)
    acc_ref[...] = jnp.zeros((ROWS, LANE), f32)
    u_ref[...] = jnp.zeros((ROWS, FEAT), f32)

    def step(chunk, _):
        cols = pl.ds(pl.multiple_of(chunk * CHUNK, CHUNK), CHUNK)
        unit = unit_ref[:, cols]
        d_ref[...] = jnp.dot(student_ref[...], unit, preferred_element_type=f32)
        for k in range(GROUPS):
            e = jnp.exp(d_ref[blk(k), :] * student_scale)
            acc_ref[blk(k), :] += e[:, :LANE] + e[:, LANE:]
            high_ref[blk(k), :], low_ref[blk(k), :] = split(e)
        u_ref[...] += nt(high_ref[...], unit) + nt(low_ref[...], unit)
        return 0

    lax.fori_loop(0, COLS // CHUNK, step, 0)
    exp_sums = jnp.concatenate([row_totals(acc_ref[blk(k), :]) for k in range(GROUPS)], axis=0)
    send_shares(msg_ref, sums, exp_sums, u_ref)


def row_pass_last(recv_ref, e_ref, student_ref, unit_ref, msg_ref, col_ref, acc_ref, dot_ref, u_ref, d_ref, high_ref, low_ref):
    col_ref[...] = 1.0 / peer_sum(recv_ref, 0, 16)
    acc_ref[...] = jnp.zeros((ROWS, LANE), f32)
    dot_ref[...] = jnp.zeros((ROWS, LANE), f32)
    u_ref[...] = jnp.zeros((ROWS, FEAT), f32)

    def step(chunk, _):
        cols = pl.ds(pl.multiple_of(chunk * CHUNK, CHUNK), CHUNK)
        unit = unit_ref[:, cols]
        d_ref[...] = jnp.dot(student_ref[...], unit, preferred_element_type=f32)
        for half in range(2):
            weight = col_ref[pl.ds(2 * chunk + half, 1), :]
            here = pl.ds(pl.multiple_of(chunk * CHUNK + half * LANE, LANE), LANE)
            for k in range(GROUPS):
                t = e_ref[blk(k), here] * weight
                acc_ref[blk(k), :] += t
                dot_ref[blk(k), :] += t * d_ref[blk(k), blk(half)]
                high_ref[blk(k), blk(half)], low_ref[blk(k), blk(half)] = split(t)
        u_ref[...] += nt(high_ref[...], unit) + nt(low_ref[...], unit)
        return 0

    lax.fori_loop(0, COLS // CHUNK, step, 0)
    sums = jnp.concatenate([row_totals(acc_ref[blk(k), :]) for k in range(GROUPS)], axis=0)
    dots = jnp.concatenate([row_totals(dot_ref[blk(k), :]) for k in range(GROUPS)], axis=0)
    send_shares(msg_ref, sums, dots * student_scale, u_ref)


def gradients(
    place_ref, last_ref, before_ref, lang_ref, count_ref, e_ref, col_ref, student_ref, unit_ref, w_ref, inv_ref, rows_ref,
    out_ref, share_ref, a_ref, b_ref, d_ref, g_ref, turned_ref,
):
    row_sum = peer_sum(last_ref, 0, 8)
    dot_sum = peer_sum(last_ref, 8, 16)
    exp_sum = peer_sum(before_ref, 8, 16)
    row_weight = 1.0 / row_sum
    target_sum = row_weight * row_sum
    cross = jnp.log(exp_sum) * target_sum - row_weight * dot_sum

    counts = count_ref[0:1, :]
    present = jnp.sum(jnp.where(counts > 0.5, 1.0, 0.0), axis=1, keepdims=True)
    count_rows = lanes(counts)
    number = lax.broadcasted_iota(jnp.int32, (LANE, LANE), 0).astype(f32)
    own = [
        jnp.sum(jnp.where(number == lang_ref[k : k + 1, :], count_rows, 0.0), axis=0, keepdims=True)
        for k in range(GROUPS)
    ]
    token_weight = 1.0 / (jnp.concatenate(own, axis=0) * present)
    loss = jnp.sum(jnp.sum(token_weight * cross, axis=1, keepdims=True), axis=0, keepdims=True)
    soft_factor = grad_scale * token_weight * target_sum / exp_sum
    target_factor = grad_scale * token_weight * row_weight
    for k in range(GROUPS):
        a_ref[blk(k), :] = lanes(soft_factor[k : k + 1, :])
        b_ref[blk(k), :] = lanes(target_factor[k : k + 1, :])
        turned_ref[:, blk(k)] = student_ref[blk(k), :].astype(f32).T.astype(bf16)

    loss_high, loss_rest = split(loss)
    loss_mid, loss_low = split(loss - loss_high.astype(f32))
    lane = lax.broadcasted_iota(jnp.int32, (FEAT, LANE), 1)
    packed = jnp.where(lane == 0, loss_high.astype(f32), jnp.where(lane == 1, loss_mid.astype(f32), loss_low.astype(f32)))
    out_ref[:, COLS : COLS + LANE] = packed.astype(bf16)

    mine = pl.ds(pl.multiple_of(place_ref[0] * SHARE, SHARE), SHARE)
    quarter = pl.ds(pl.multiple_of(place_ref[1] * SHARE, SHARE), SHARE)
    a, b = a_ref[mine, :], b_ref[mine, :]
    grads = [
        student_scale
        * (
            a * peer_sum(before_ref, 16 + part * SHARE, 16 + (part + 1) * SHARE)
            - b * peer_sum(last_ref, 16 + part * SHARE, 16 + (part + 1) * SHARE)
        )
        for part in range(2)
    ]
    grad_unit = jnp.concatenate(grads, axis=1)
    rows = rows_ref[quarter, :]
    row_inv = unit_inverse(rows)
    along = jnp.sum(rows * grad_unit, axis=1, keepdims=True)
    share_ref[...] = row_inv * grad_unit - rows * (row_inv * row_inv * row_inv) * along

    def step(chunk, _):
        cols = pl.ds(pl.multiple_of(chunk * CHUNK, CHUNK), CHUNK)
        d_ref[...] = jnp.dot(student_ref[...], unit_ref[:, cols], preferred_element_type=f32)
        for half in range(2):
            weight = col_ref[pl.ds(2 * chunk + half, 1), :]
            here = pl.ds(pl.multiple_of(chunk * CHUNK + half * LANE, LANE), LANE)
            for k in range(GROUPS):
                soft = a_ref[blk(k), :] * jnp.exp(d_ref[blk(k), blk(half)] * student_scale)
                target = b_ref[blk(k), :] * e_ref[blk(k), here] * weight
                g_ref[blk(k), blk(half)] = (soft - target).astype(bf16)
        full = jnp.dot(turned_ref[...], g_ref[...], preferred_element_type=f32) * student_scale
        w = w_ref[:, cols].astype(f32)
        inv = inv_ref[:, cols]
        inner = jnp.sum(w * full, axis=0, keepdims=True)
        out_ref[:, cols] = (inv * full - w * (inv * inv * inv * inner)).astype(bf16)
        return 0

    lax.fori_loop(0, COLS // CHUNK, step, 0)


def scatter_rows(place_ref, pos_ref, own_ref, one_ref, two_ref, three_ref, out_ref, all_ref):
    for shift, ref in enumerate((own_ref, one_ref, two_ref, three_ref)):
        quarter = lax.rem(place_ref[1] - shift + Y, Y)
        all_ref[pl.ds(pl.multiple_of(quarter * SHARE, SHARE), SHARE), :] = ref[...]
    where = lax.broadcasted_iota(jnp.int32, (FEAT, TOK), 0) == pos_ref[...]
    picker = jnp.where(where, 1.0, 0.0).astype(bf16)
    rows = all_ref[...]
    high, _ = split(rows)
    mid, low = split(rows - high.astype(f32))
    out_ref[...] = (
        jnp.dot(picker, high, preferred_element_type=f32)
        + jnp.dot(picker, mid, preferred_element_type=f32)
        + jnp.dot(picker, low, preferred_element_type=f32)
    )


def add_groups(recv_ref, out_ref, loss_ref):
    for group in range(GROUPS):
        total = recv_ref[group, :, 0:COLS].astype(f32)
        for z in range(1, Z):
            total = total + recv_ref[z * GROUPS + group, :, 0:COLS].astype(f32)
        out_ref[:, group * COLS : (group + 1) * COLS] = total
    loss = recv_ref[0, :, COLS : COLS + LANE].astype(f32)
    for z in range(1, Z):
        loss = loss + recv_ref[z * GROUPS, :, COLS : COLS + LANE].astype(f32)
    lane = lax.broadcasted_iota(jnp.int32, loss.shape, 1)
    loss_ref[...] = jnp.sum(jnp.where(lane < 3, loss, 0.0)[0:1, :], axis=1, keepdims=True)


def exchange(message, axes):
    return lax.all_to_all(message, axes, 0, 0)


def local(teacher_seq, student_seq, prototypes, positions, languages):
    shape = jax.ShapeDtypeStruct
    kept = pltpu.VMEM
    z_axis, row_axes, tok_axes = ("z",), ("x", "c", "y"), ("z", "x", "c")
    group = lax.axis_index("x") * C + lax.axis_index("c")
    y = lax.axis_index("y")
    place = jnp.stack([group * Y + y, y]).astype(jnp.int32)
    w = lax.dynamic_slice_in_dim(prototypes, group * COLS, COLS, axis=1)
    pos = positions[None, :]

    units, rows = call(pick_rows, (shape((GROUPS, TOK + 16, 2 * FEAT), bf16), shape((TOK, FEAT), f32)))(
        pos, languages[None, :], teacher_seq, student_seq
    )
    units = exchange(units, ("x", "c"))
    e, unit, inv, student, lang, count, message = call(
        start,
        (
            kept((ROWS, COLS), f32),
            kept((FEAT, COLS), bf16),
            shape((1, COLS), f32),
            kept((ROWS, FEAT), bf16),
            shape((8, LANE), f32),
            shape((8, LANE), f32),
            shape((PEERS, 8, LANE), f32),
        ),
        [pltpu.VMEM((ROWS, FEAT), bf16), pltpu.VMEM((ROWS, LANE), f32), pltpu.VMEM((ROWS, CHUNK), f32)],
    )(units, w)

    work = [
        pltpu.VMEM((ROWS, FEAT), f32),
        pltpu.VMEM((ROWS, CHUNK), f32),
        pltpu.VMEM((ROWS, CHUNK), bf16),
        pltpu.VMEM((ROWS, CHUNK), bf16),
    ]
    totals = pltpu.VMEM((ROWS, LANE), f32)
    shares = shape((PEERS, 16 + 2 * SHARE, LANE), f32)
    counts = None
    for sweep in range(ITERS):
        received = exchange(message, row_axes)
        if sweep == ITERS - 1:
            before = received
        out = shape((Z, 24 if sweep == 0 else 16, LANE), f32)
        message = call(column_pass, out, [pltpu.VMEM((COLS // LANE, 8, LANE), f32)])(received, e, count)
        received = exchange(message, z_axis)
        if sweep < ITERS - 2:
            message, counts = call(row_pass, (shape((PEERS, 8, LANE), f32), shape((8, LANE), f32)))(received, e)
        elif sweep == ITERS - 2:
            message = call(row_pass_student, shares, [totals] + work)(received, e, student, unit)
        else:
            message, col = call(row_pass_last, (shares, shape((16, LANE), f32)), [totals, totals] + work)(
                received, e, student, unit
            )
    last = exchange(message, row_axes)
    grad, share = call(
        gradients,
        (shape((FEAT, COLS + LOSS_LANES), bf16), shape((SHARE, FEAT), f32)),
        [
            totals,
            totals,
            pltpu.VMEM((ROWS, CHUNK), f32),
            pltpu.VMEM((ROWS, CHUNK), bf16),
            pltpu.VMEM((FEAT, ROWS), bf16),
        ],
        smem_first=True,
    )(place, last, before, lang, counts, e, col, student, unit, w, inv, rows)
    others = [lax.ppermute(share, "y", [(i, (i + s) % Y) for i in range(Y)]) for s in range(1, Y)]
    grad = exchange(grad.reshape(Z * GROUPS, 4, COLS + LOSS_LANES), tok_axes)
    grad_student = call(scatter_rows, shape((FEAT, FEAT), f32), [pltpu.VMEM((TOK, FEAT), f32)], smem_first=True)(
        place, pos, share, *others
    )
    grad_prototypes, loss = call(add_groups, (shape((4, GROUPS * COLS), f32), shape((1, 1), f32)))(grad)
    return (loss[0, 0], grad_student, grad_prototypes)


def solution(mesh):
    fine = Mesh(mesh.devices.reshape(Z, X, C, Y), ("z", "x", "c", "y"))
    tok = ("z", "x", "c")
    in_specs = (P(tok, None), P(tok, None), P(None, "y"), P(tok), P(tok))
    out_specs = (P(), P(tok, None), P(tok, "y"))
    return jax.shard_map(local, mesh=fine, in_specs=in_specs, out_specs=out_specs, check_vma=False)
```

```python
import jax
import jax.numpy as jnp
from jax import lax
from jax.experimental import pallas as pl
from jax.experimental.pallas import tpu as pltpu
from jax.sharding import Mesh, PartitionSpec as P

LANGS = 100
ITERS = 3

epsilon = 1e-06
teacher_scale = 20.0
student_scale = 10.0
grad_scale = 8388608.0

Z, X, C, Y = 8, 4, 2, 4
TOK = 128
GROUPS = X * C
ROWS = GROUPS * TOK
COLS = 2048
FEAT = 256
LANE = 128
CHUNK = 512
PARTS = CHUNK // LANE
PEERS = X * C * Y
SHARE = ROWS // PEERS
LOSS_LANES = 128
f32 = jnp.float32
bf16 = jnp.bfloat16


def call(kernel, out_shape, scratch=(), anywhere=(), out_anywhere=(), flops=0, mib=20):
    def run(*args):
        space = lambda far: pl.BlockSpec(memory_space=pltpu.HBM if far else pltpu.VMEM)
        multiple = isinstance(out_shape, (tuple, list))
        outs = [space(i in out_anywhere) for i in range(len(out_shape) if multiple else 1)]
        return pl.pallas_call(
            kernel,
            out_shape=out_shape,
            in_specs=[space(i in anywhere) for i in range(len(args))],
            out_specs=outs if multiple else outs[0],
            scratch_shapes=list(scratch),
            compiler_params=pltpu.CompilerParams(vmem_limit_bytes=mib << 20),
            cost_estimate=pl.CostEstimate(flops=flops, bytes_accessed=1 << 20, transcendentals=0),
            name=kernel.__name__,
        )(*args)

    return run


def lanes(row):
    return jnp.broadcast_to(row, (LANE, LANE)).T


def row_totals(block):
    return jnp.sum(block.T, axis=0, keepdims=True)


def blk(index):
    return pl.ds(index * LANE, LANE)


def split(values):
    high = values.astype(bf16)
    return high, (values - high.astype(f32)).astype(bf16)


def nt(left, right):
    return lax.dot_general(left, right, (((1,), (1,)), ((), ())), preferred_element_type=f32)


def tn(left, right):
    return lax.dot_general(left, right, (((0,), (0,)), ((), ())), preferred_element_type=f32)


def unit_inverse(values):
    return lax.rsqrt(jnp.sum(values * values, axis=1, keepdims=True) + epsilon)


def fetch(sources, targets, sems):
    copies = [pltpu.make_async_copy(a, b, sems.at[n]) for n, (a, b) in enumerate(zip(sources, targets))]
    for copy in copies:
        copy.start()
    for copy in copies:
        copy.wait()


def pick_rows(pos_hbm, lang_hbm, teacher_hbm, student_hbm, out_ref, rows_ref, pos_ref, lang_ref, teacher_ref, student_ref, sems):
    fetch((pos_hbm, lang_hbm, teacher_hbm, student_hbm), (pos_ref, lang_ref, teacher_ref, student_ref), sems)
    where = lax.broadcasted_iota(jnp.int32, (FEAT, TOK), 0) == pos_ref[...]
    picker = jnp.where(where, 1.0, 0.0).astype(bf16)
    teacher = tn(picker, teacher_ref[...])
    student = tn(picker, student_ref[...])
    teacher_unit = (teacher * unit_inverse(teacher)).astype(bf16)
    student_unit = (student * unit_inverse(student)).astype(bf16)
    language = jnp.broadcast_to(lang_ref[...].astype(f32), (16, TOK)).astype(bf16)
    rows_ref[...] = student
    for peer in range(X):
        out_ref[peer, 0:TOK, 0:FEAT] = teacher_unit
        out_ref[peer, 0:TOK, FEAT : 2 * FEAT] = student_unit
        for part in range(4):
            out_ref[peer, TOK : TOK + 16, part * LANE : (part + 1) * LANE] = language


def weights(proto_hbm, w_ref, unit_ref, inv_ref, sems):
    group = lax.axis_index("x") * C + lax.axis_index("c")
    here = pl.ds(pl.multiple_of(group * COLS, COLS), COLS)
    fetch((proto_hbm.at[:, here],), (w_ref,), sems)
    for chunk in range(COLS // CHUNK):
        cols = pl.ds(chunk * CHUNK, CHUNK)
        w = w_ref[:, cols].astype(f32)
        inv = lax.rsqrt(jnp.sum(w * w, axis=0, keepdims=True) + epsilon)
        inv_ref[:, cols] = inv
        unit_ref[:, cols] = (w * inv).astype(bf16)


def chunk_cols(chunk):
    return pl.ds(pl.multiple_of(chunk * CHUNK, CHUNK), CHUNK)


def lane_sum(block):
    total = block[:, 0:LANE]
    for part in range(1, PARTS):
        total = total + block[:, part * LANE : (part + 1) * LANE]
    return total


def all_row_totals(acc_ref):
    return jnp.concatenate([row_totals(acc_ref[blk(k), :]) for k in range(GROUPS)], axis=0)


def start(own_ref, other_ref, unit_ref, teacher_ref, student_ref, lang_ref, count_ref, msg_ref, acc_ref, d_ref):
    core = lax.axis_index("c")
    for x in range(X):
        for ref, c in ((own_ref, core), (other_ref, 1 - core)):
            here = pl.ds(pl.multiple_of((x * C + c) * TOK, TOK), TOK)
            teacher_ref[here, :] = ref[x, 0:TOK, 0:FEAT]
            student_ref[here, :] = ref[x, 0:TOK, FEAT : 2 * FEAT]
            lang_ref[pl.ds(x * C + c, 1), :] = ref[x, TOK : TOK + 16, 0:LANE].astype(f32)[0:1, :]
    hits = jnp.zeros((LANE, LANE), f32)
    number = lax.broadcasted_iota(jnp.int32, (LANE, LANE), 0).astype(f32)
    for k in range(GROUPS):
        hits = hits + jnp.where(number == lang_ref[k : k + 1, :], 1.0, 0.0)
    count_ref[...] = jnp.broadcast_to(row_totals(hits), (8, LANE))
    acc_ref[...] = jnp.zeros((ROWS, LANE), f32)

    def step(chunk, _):
        d_ref[...] = jnp.dot(teacher_ref[...], unit_ref[:, chunk_cols(chunk)], preferred_element_type=f32)
        for k in range(GROUPS):
            acc_ref[blk(k), :] += lane_sum(jnp.exp(d_ref[blk(k), :] * teacher_scale))
        return 0

    lax.fori_loop(0, COLS // CHUNK, step, 0)
    sums = all_row_totals(acc_ref)
    for peer in range(PEERS):
        msg_ref[peer] = sums


def two_parts(values):
    high, low = split(values)
    return jnp.concatenate([high.astype(f32), low.astype(f32)], axis=0).astype(bf16)


def write_shares(msg_ref, low, stat, u_ref):
    for peer in range(PEERS):
        msg_ref[peer, low : low + 16, :] = stat
        share = u_ref[pl.ds(peer * SHARE, SHARE), :].astype(bf16)
        msg_ref[peer, low + 16 : low + 16 + SHARE, :] = share[:, 0:LANE]
        msg_ref[peer, low + 16 + SHARE : low + 16 + 2 * SHARE, :] = share[:, LANE : 2 * LANE]


def student_pass(student_ref, unit_ref, msg_ref, turned_ref, acc_ref, u_ref, d_ref, g_ref):
    for k in range(GROUPS):
        turned_ref[:, blk(k)] = student_ref[blk(k), :].astype(f32).T.astype(bf16)
    acc_ref[...] = jnp.zeros((ROWS, LANE), f32)
    u_ref[...] = jnp.zeros((ROWS, FEAT), f32)

    def step(chunk, _):
        unit = unit_ref[:, chunk_cols(chunk)]
        d_ref[...] = jnp.dot(student_ref[...], unit, preferred_element_type=f32)
        for k in range(GROUPS):
            e = jnp.exp(d_ref[blk(k), :] * student_scale)
            acc_ref[blk(k), :] += lane_sum(e)
            g_ref[blk(k), :] = e.astype(bf16)
        u_ref[...] += nt(g_ref[...], unit)
        return 0

    lax.fori_loop(0, COLS // CHUNK, step, 0)
    write_shares(msg_ref, 0, two_parts(all_row_totals(acc_ref)), u_ref)


def peer_sum(recv_ref, low, high):
    total = recv_ref[0, low:high, :].astype(f32)
    for peer in range(1, recv_ref.shape[0]):
        total = total + recv_ref[peer, low:high, :].astype(f32)
    return total


def row_sums(recv_ref, low=0):
    if recv_ref.dtype == f32:
        return peer_sum(recv_ref, low, low + 8)
    both = peer_sum(recv_ref, low, low + 16)
    return both[0:8] + both[8:16]


def column_first(recv_ref, teacher_ref, unit_ref, count_ref, e_ref, msg_ref, factor_ref, sum_ref, d_ref):
    row_weight = 1.0 / row_sums(recv_ref)
    for k in range(GROUPS):
        factor_ref[blk(k), :] = lanes(row_weight[k : k + 1, :])

    def step(chunk, _):
        cols = chunk_cols(chunk)
        d_ref[...] = jnp.dot(teacher_ref[...], unit_ref[:, cols], preferred_element_type=f32)
        total = [jnp.zeros((8, LANE), f32)] * PARTS
        for k in range(GROUPS):
            e = jnp.exp(d_ref[blk(k), :] * teacher_scale)
            e_ref[blk(k), cols] = e
            factor = factor_ref[blk(k), :]
            for part in range(PARTS):
                scaled = e[:, part * LANE : (part + 1) * LANE] * factor
                total[part] = total[part] + jnp.sum(scaled.reshape(LANE // 8, 8, LANE), axis=0)
        for part in range(PARTS):
            sum_ref[pl.ds(chunk * PARTS + part, 1), :] = jnp.sum(total[part], axis=0, keepdims=True)
        return 0

    lax.fori_loop(0, COLS // CHUNK, step, 0)
    for peer in range(Z):
        msg_ref[peer, 0:16, :] = sum_ref[...]
        msg_ref[peer, 16:24, :] = count_ref[...]


def column_pass(recv_ref, e_ref, msg_ref, acc_ref):
    row_weight = 1.0 / row_sums(recv_ref)
    for k in range(GROUPS):
        factor = lanes(row_weight[k : k + 1, :])
        for j in range(COLS // LANE):
            part = jnp.sum((e_ref[blk(k), blk(j)] * factor).reshape(LANE // 8, 8, LANE), axis=0)
            acc_ref[j] = part if k == 0 else acc_ref[j] + part
    sums = jnp.concatenate([jnp.sum(acc_ref[j], axis=0, keepdims=True) for j in range(COLS // LANE)], axis=0)
    for peer in range(Z):
        msg_ref[peer] = sums


def weighted_rows(e_ref, col_weight):
    out = []
    for k in range(GROUPS):
        acc = e_ref[blk(k), blk(0)] * col_weight[0:1, :]
        for j in range(1, COLS // LANE):
            acc = acc + e_ref[blk(k), blk(j)] * col_weight[j : j + 1, :]
        out.append(row_totals(acc))
    return jnp.concatenate(out, axis=0)


def row_first(recv_ref, e_ref, msg_ref, count_ref):
    count_ref[...] = peer_sum(recv_ref, 16, 24)
    sums = weighted_rows(e_ref, 1.0 / peer_sum(recv_ref, 0, 16))
    for peer in range(PEERS):
        msg_ref[peer] = sums


def row_pass(recv_ref, e_ref, stat_ref, msg_ref):
    sums = two_parts(weighted_rows(e_ref, 1.0 / peer_sum(recv_ref, 0, 16)))
    for peer in range(PEERS):
        msg_ref[peer, 0:16, :] = sums
        msg_ref[peer, 16:96, :] = stat_ref[peer]


def row_last(recv_ref, e_ref, student_ref, unit_ref, msg_ref, col_ref, acc_ref, dot_ref, u_ref, d_ref, g_ref):
    col_ref[...] = 1.0 / peer_sum(recv_ref, 0, 16)
    acc_ref[...] = jnp.zeros((ROWS, LANE), f32)
    dot_ref[...] = jnp.zeros((ROWS, LANE), f32)
    u_ref[...] = jnp.zeros((ROWS, FEAT), f32)

    def step(chunk, _):
        unit = unit_ref[:, chunk_cols(chunk)]
        d_ref[...] = jnp.dot(student_ref[...], unit, preferred_element_type=f32)
        weight = [col_ref[pl.ds(chunk * PARTS + part, 1), :] for part in range(PARTS)]
        for k in range(GROUPS):
            total, dot = acc_ref[blk(k), :], dot_ref[blk(k), :]
            for part in range(PARTS):
                here = pl.ds(pl.multiple_of(chunk * CHUNK + part * LANE, LANE), LANE)
                t = e_ref[blk(k), here] * weight[part]
                total = total + t
                dot = dot + t * d_ref[blk(k), blk(part)]
                g_ref[blk(k), blk(part)] = t.astype(bf16)
            acc_ref[blk(k), :] = total
            dot_ref[blk(k), :] = dot
        u_ref[...] += nt(g_ref[...], unit)
        return 0

    lax.fori_loop(0, COLS // CHUNK, step, 0)
    sums = two_parts(all_row_totals(acc_ref))
    for peer in range(PEERS):
        msg_ref[peer, 0:16, :] = sums
    write_shares(msg_ref, 16, two_parts(all_row_totals(dot_ref) * student_scale), u_ref)


def gradients(
    last_ref, before_ref, lang_ref, count_ref, e_ref, col_ref, student_ref, turned_ref, unit_ref, w_ref, inv_ref, rows_ref,
    out_hbm, share_ref, a_ref, b_ref, d_ref, g_ref, out_ref, sems,
):
    y = lax.axis_index("y")
    group = lax.axis_index("x") * C + lax.axis_index("c")
    row_sum = row_sums(last_ref)
    dot_sum = row_sums(last_ref, 16)
    exp_sum = row_sums(before_ref, 16)
    row_weight = 1.0 / row_sum
    target_sum = row_weight * row_sum
    cross = jnp.log(exp_sum) * target_sum - row_weight * dot_sum

    counts = count_ref[0:1, :]
    present = jnp.sum(jnp.where(counts > 0.5, 1.0, 0.0), axis=1, keepdims=True)
    count_rows = lanes(counts)
    number = lax.broadcasted_iota(jnp.int32, (LANE, LANE), 0).astype(f32)
    own = [
        jnp.sum(jnp.where(number == lang_ref[k : k + 1, :], count_rows, 0.0), axis=0, keepdims=True)
        for k in range(GROUPS)
    ]
    token_weight = 1.0 / (jnp.concatenate(own, axis=0) * present)
    loss = jnp.sum(jnp.sum(token_weight * cross, axis=1, keepdims=True), axis=0, keepdims=True)
    soft_factor = grad_scale * token_weight * target_sum / exp_sum
    target_factor = grad_scale * token_weight * row_weight
    for k in range(GROUPS):
        a_ref[blk(k), :] = lanes(soft_factor[k : k + 1, :])
        b_ref[blk(k), :] = lanes(target_factor[k : k + 1, :])

    def send(chunk, width):
        cols = pl.ds(pl.multiple_of(chunk * CHUNK, CHUNK), width)
        return pltpu.make_async_copy(out_ref.at[:, cols], out_hbm.at[:, cols], sems.at[chunk])

    loss_high, _ = split(loss)
    loss_mid, loss_low = split(loss - loss_high.astype(f32))
    lane = lax.broadcasted_iota(jnp.int32, (FEAT, LANE), 1)
    packed = jnp.where(lane == 0, loss_high.astype(f32), jnp.where(lane == 1, loss_mid.astype(f32), loss_low.astype(f32)))
    out_ref[:, COLS : COLS + LANE] = packed.astype(bf16)
    send(COLS // CHUNK, LOSS_LANES).start()

    mine = pl.ds(pl.multiple_of((group * Y + y) * SHARE, SHARE), SHARE)
    quarter = pl.ds(pl.multiple_of(y * SHARE, SHARE), SHARE)
    a, b = a_ref[mine, :], b_ref[mine, :]
    grads = [
        student_scale
        * (
            a * peer_sum(before_ref, 32 + part * SHARE, 32 + (part + 1) * SHARE)
            - b * peer_sum(last_ref, 32 + part * SHARE, 32 + (part + 1) * SHARE)
        )
        for part in range(2)
    ]
    grad_unit = jnp.concatenate(grads, axis=1)
    rows = rows_ref[quarter, :]
    row_inv = unit_inverse(rows)
    along = jnp.sum(rows * grad_unit, axis=1, keepdims=True)
    share_ref[...] = row_inv * grad_unit - rows * (row_inv * row_inv * row_inv) * along

    def step(chunk, _):
        cols = chunk_cols(chunk)
        d_ref[...] = jnp.dot(student_ref[...], unit_ref[:, cols], preferred_element_type=f32)
        weight = [col_ref[pl.ds(chunk * PARTS + part, 1), :] for part in range(PARTS)]
        for k in range(GROUPS):
            a, b = a_ref[blk(k), :], b_ref[blk(k), :]
            for part in range(PARTS):
                here = pl.ds(pl.multiple_of(chunk * CHUNK + part * LANE, LANE), LANE)
                soft = a * jnp.exp(d_ref[blk(k), blk(part)] * student_scale)
                target = b * e_ref[blk(k), here] * weight[part]
                g_ref[blk(k), blk(part)] = (soft - target).astype(bf16)
        full = jnp.dot(turned_ref[...], g_ref[...], preferred_element_type=f32) * student_scale
        w = w_ref[:, cols].astype(f32)
        inv = inv_ref[:, cols]
        inner = jnp.sum(w * full, axis=0, keepdims=True)
        out_ref[:, cols] = (inv * full - w * (inv * inv * inv * inner)).astype(bf16)
        send(chunk, CHUNK).start()
        return 0

    lax.fori_loop(0, COLS // CHUNK, step, 0)
    for chunk in range(COLS // CHUNK):
        send(chunk, CHUNK).wait()
    send(COLS // CHUNK, LOSS_LANES).wait()


def scatter_rows(pos_hbm, own_ref, one_ref, two_ref, three_ref, out_ref, all_ref, pos_ref, sems):
    fetch((pos_hbm,), (pos_ref,), sems)
    y = lax.axis_index("y")
    for shift, ref in enumerate((own_ref, one_ref, two_ref, three_ref)):
        quarter = lax.rem(y - shift + Y, Y)
        all_ref[pl.ds(pl.multiple_of(quarter * SHARE, SHARE), SHARE), :] = ref[...]
    where = lax.broadcasted_iota(jnp.int32, (FEAT, TOK), 0) == pos_ref[...]
    picker = jnp.where(where, 1.0, 0.0).astype(bf16)
    rows = all_ref[...]
    high, _ = split(rows)
    mid, low = split(rows - high.astype(f32))
    out_ref[...] = (
        jnp.dot(picker, high, preferred_element_type=f32)
        + jnp.dot(picker, mid, preferred_element_type=f32)
        + jnp.dot(picker, low, preferred_element_type=f32)
    )


def add_groups(recv_ref, own_ref, other_ref, loss_ref):
    first = lax.axis_index("c") == 0
    for x in range(X):
        for chunk in range(COLS // CHUNK):
            cols = pl.ds(chunk * CHUNK, CHUNK)
            total = recv_ref[x, :, cols].astype(f32)
            for z in range(1, Z):
                total = total + recv_ref[z * X + x, :, cols].astype(f32)
            there = pl.ds(x * COLS + chunk * CHUNK, CHUNK)
            own_ref[:, there] = jnp.where(first, total[0:4], total[4:8])
            other_ref[:, there] = jnp.where(first, total[4:8], total[0:4])
    loss = recv_ref[0, :, COLS : COLS + LANE].astype(f32)
    for z in range(1, Z):
        loss = loss + recv_ref[z * X, :, COLS : COLS + LANE].astype(f32)
    lane = lax.broadcasted_iota(jnp.int32, loss.shape, 1)
    loss_ref[...] = jnp.sum(jnp.where(lane < 3, loss, 0.0)[0:1, :], axis=1, keepdims=True)


def join(own_ref, other_ref, out_ref):
    core = lax.axis_index("c")
    for x in range(X):
        for ref, c in ((own_ref, core), (other_ref, 1 - core)):
            there = pl.ds(pl.multiple_of((x * C + c) * COLS, COLS), COLS)
            out_ref[:, there] = ref[:, x * COLS : (x + 1) * COLS]


def exchange(message, axes):
    return lax.all_to_all(message, axes, 0, 0)


def other_core(values):
    return lax.ppermute(values, "c", [(0, 1), (1, 0)])


def local(teacher_seq, student_seq, prototypes, positions, languages):
    shape = jax.ShapeDtypeStruct
    kept = pltpu.VMEM
    sems = pltpu.SemaphoreType.DMA
    z_axis, row_axes = ("z",), ("x", "c", "y")
    pos = positions[None, :]
    pass_flops = 2 * ROWS * COLS * FEAT

    units, rows = call(
        pick_rows,
        (shape((X, TOK + 16, 2 * FEAT), bf16), shape((TOK, FEAT), f32)),
        [
            pltpu.VMEM((1, TOK), jnp.int32),
            pltpu.VMEM((1, TOK), jnp.int32),
            pltpu.VMEM((FEAT, FEAT), bf16),
            pltpu.VMEM((FEAT, FEAT), bf16),
            sems((4,)),
        ],
        anywhere=(0, 1, 2, 3),
    )(pos, languages[None, :], teacher_seq, student_seq)
    w, unit, inv = call(
        weights,
        (shape((FEAT, COLS), bf16), shape((FEAT, COLS), bf16), shape((1, COLS), f32)),
        [sems((1,))],
        anywhere=(0,),
        flops=pass_flops,
    )(prototypes)
    units = exchange(units, ("x",))
    teacher, student, lang, count, message = call(
        start,
        (
            shape((ROWS, FEAT), bf16),
            shape((ROWS, FEAT), bf16),
            shape((8, LANE), f32),
            shape((8, LANE), f32),
            shape((PEERS, 8, LANE), f32),
        ),
        [pltpu.VMEM((ROWS, LANE), f32), pltpu.VMEM((ROWS, CHUNK), f32)],
    )(units, other_core(units), unit)

    totals = pltpu.VMEM((ROWS, LANE), f32)
    products = pltpu.VMEM((ROWS, CHUNK), f32)
    rounded = pltpu.VMEM((ROWS, CHUNK), bf16)
    features = pltpu.VMEM((ROWS, FEAT), f32)
    received = exchange(message, row_axes)
    stats, turned = call(
        student_pass,
        (shape((PEERS, 16 + 2 * SHARE, LANE), bf16), shape((FEAT, ROWS), bf16)),
        [totals, features, products, rounded],
        flops=4 * pass_flops,
    )(student, unit)
    received, stats, turned = lax.optimization_barrier((received, stats, turned))
    e, message = call(
        column_first,
        (kept((ROWS, COLS), f32), shape((Z, 24, LANE), f32)),
        [totals, pltpu.VMEM((16, LANE), f32), products],
    )(received, teacher, unit, count)
    message, counts = call(row_first, (shape((PEERS, 8, LANE), f32), shape((8, LANE), f32)))(exchange(message, z_axis), e)
    column = call(column_pass, shape((Z, 16, LANE), f32), [pltpu.VMEM((COLS // LANE, 8, LANE), f32)])
    full = shape((PEERS, 32 + 2 * SHARE, LANE), bf16)
    for sweep in range(1, ITERS):
        received = exchange(message, row_axes)
        columns = exchange(column(received, e), z_axis)
        if sweep < ITERS - 1:
            message = call(row_pass, full)(columns, e, stats)
        else:
            message, col = call(
                row_last, (full, shape((16, LANE), f32)), [totals, totals, features, products, rounded]
            )(columns, e, student, unit)
    last = exchange(message, row_axes)
    grad, share = call(
        gradients,
        (pltpu.HBM((FEAT, COLS + LOSS_LANES), bf16), shape((SHARE, FEAT), f32)),
        [
            totals,
            totals,
            products,
            rounded,
            pltpu.VMEM((FEAT, COLS + LOSS_LANES), bf16),
            sems((COLS // CHUNK + 1,)),
        ],
        out_anywhere=(0,),
    )(last, received, lang, counts, e, col, student, turned, unit, w, inv, rows)
    others = [lax.ppermute(share, "y", [(i, (i + s) % Y) for i in range(Y)]) for s in range(1, Y)]
    grad = exchange(grad.reshape(Z * X, 8, COLS + LOSS_LANES), ("z", "x"))
    grad_student = call(
        scatter_rows,
        shape((FEAT, FEAT), f32),
        [pltpu.VMEM((TOK, FEAT), f32), pltpu.VMEM((1, TOK), jnp.int32), sems((1,))],
        anywhere=(0,),
    )(pos, share, *others)
    grad, grad_student = lax.optimization_barrier((grad, grad_student))
    half = shape((4, X * COLS), f32)
    mine, theirs, loss = call(add_groups, (half, half, shape((1, 1), f32)))(grad)
    grad_prototypes = call(join, shape((4, GROUPS * COLS), f32))(mine, other_core(theirs))
    return (loss[0, 0], grad_student, grad_prototypes)


def solution(mesh):
    fine = Mesh(mesh.devices.reshape(Z, X, C, Y), ("z", "x", "c", "y"))
    tok = ("z", "x", "c")
    in_specs = (P(tok, None), P(tok, None), P(None, "y"), P(tok), P(tok))
    out_specs = (P(), P(tok, None), P(tok, "y"))
    return jax.shard_map(local, mesh=fine, in_specs=in_specs, out_specs=out_specs, check_vma=False)
```

```python
import jax
import jax.numpy as jnp
from jax import lax
from jax.experimental import pallas as pl
from jax.experimental.pallas import tpu as pltpu
from jax.sharding import Mesh, PartitionSpec as P

LANGS = 100
ITERS = 3

epsilon = 1e-06
teacher_scale = 20.0
student_scale = 10.0
grad_scale = 8388608.0

Z, X, C, Y = 8, 4, 2, 4
TOK = 128
GROUPS = X * C
ROWS = GROUPS * TOK
COLS = 2048
FEAT = 256
LANE = 128
CHUNK = 512
PARTS = CHUNK // LANE
PEERS = X * C * Y
LOSS_LANES = 128
f32 = jnp.float32
bf16 = jnp.bfloat16


def call(kernel, out_shape, scratch=(), anywhere=(), out_anywhere=(), mib=24):
    def run(*args):
        space = lambda far: pl.BlockSpec(memory_space=pltpu.HBM if far else pltpu.VMEM)
        args = [pltpu.with_memory_space_constraint(a, pltpu.HBM) if i in anywhere else a for i, a in enumerate(args)]
        multiple = isinstance(out_shape, (tuple, list))
        outs = [space(i in out_anywhere) for i in range(len(out_shape) if multiple else 1)]
        return pl.pallas_call(
            kernel,
            out_shape=out_shape,
            in_specs=[space(i in anywhere) for i in range(len(args))],
            out_specs=outs if multiple else outs[0],
            scratch_shapes=list(scratch),
            compiler_params=pltpu.CompilerParams(vmem_limit_bytes=mib << 20),
            name=kernel.__name__,
        )(*args)

    return run


def lanes(row):
    return jnp.broadcast_to(row, (LANE, LANE)).T


def row_totals(block):
    return jnp.sum(block.T, axis=0, keepdims=True)


def blk(index):
    return pl.ds(index * LANE, LANE)


def split(values):
    high = values.astype(bf16)
    return high, (values - high.astype(f32)).astype(bf16)


def nt(left, right):
    return lax.dot_general(left, right, (((1,), (1,)), ((), ())), preferred_element_type=f32)


def tn(left, right):
    return lax.dot_general(left, right, (((0,), (0,)), ((), ())), preferred_element_type=f32)


def unit_inverse(values):
    return lax.rsqrt(jnp.sum(values * values, axis=1, keepdims=True) + epsilon)


def fetch(sources, targets, sems):
    copies = [pltpu.make_async_copy(a, b, sems.at[n]) for n, (a, b) in enumerate(zip(sources, targets))]
    for copy in copies:
        copy.start()
    for copy in copies:
        copy.wait()


def pick_rows(pos_hbm, lang_hbm, teacher_hbm, student_hbm, out_ref, rows_ref, pos_ref, lang_ref, teacher_ref, student_ref, sems):
    fetch((pos_hbm, lang_hbm, teacher_hbm, student_hbm), (pos_ref, lang_ref, teacher_ref, student_ref), sems)
    where = lax.broadcasted_iota(jnp.int32, (FEAT, TOK), 0) == pos_ref[...]
    picker = jnp.where(where, 1.0, 0.0).astype(bf16)
    teacher = tn(picker, teacher_ref[...])
    student = tn(picker, student_ref[...])
    teacher_unit = (teacher * unit_inverse(teacher)).astype(bf16)
    student_unit = (student * unit_inverse(student)).astype(bf16)
    language = jnp.broadcast_to(lang_ref[...].astype(f32), (16, TOK)).astype(bf16)
    rows_ref[...] = student
    for peer in range(X):
        out_ref[peer, 0:TOK, 0:FEAT] = teacher_unit
        out_ref[peer, 0:TOK, FEAT : 2 * FEAT] = student_unit
        for part in range(4):
            out_ref[peer, TOK : TOK + 16, part * LANE : (part + 1) * LANE] = language


def weights(proto_hbm, w_ref, unit_ref, inv_ref, sems):
    group = lax.axis_index("x") * C + lax.axis_index("c")
    here = pl.ds(pl.multiple_of(group * COLS, COLS), COLS)
    fetch((proto_hbm.at[:, here],), (w_ref,), sems)
    for chunk in range(COLS // CHUNK):
        cols = pl.ds(chunk * CHUNK, CHUNK)
        w = w_ref[:, cols].astype(f32)
        inv = lax.rsqrt(jnp.sum(w * w, axis=0, keepdims=True) + epsilon)
        inv_ref[:, cols] = inv
        unit_ref[:, cols] = (w * inv).astype(bf16)


def chunk_cols(chunk):
    return pl.ds(pl.multiple_of(chunk * CHUNK, CHUNK), CHUNK)


def lane_sum(block):
    total = block[:, 0:LANE]
    for part in range(1, PARTS):
        total = total + block[:, part * LANE : (part + 1) * LANE]
    return total


def all_row_totals(acc_ref):
    return jnp.concatenate([row_totals(acc_ref[blk(k), :]) for k in range(GROUPS)], axis=0)


def start(
    own_ref, other_ref, unit_ref, e_ref, student_ref, turned_ref, lang_ref, count_ref, msg_ref,
    teacher_ref, acc_ref, exp_ref, d_ref, l_ref,
):
    core = lax.axis_index("c")
    for x in range(X):
        for ref, c in ((own_ref, core), (other_ref, 1 - core)):
            here = pl.ds(pl.multiple_of((x * C + c) * TOK, TOK), TOK)
            teacher_ref[here, :] = ref[x, 0:TOK, 0:FEAT]
            student_ref[here, :] = ref[x, 0:TOK, FEAT : 2 * FEAT]
            lang_ref[pl.ds(x * C + c, 1), :] = ref[x, TOK : TOK + 16, 0:LANE].astype(f32)[0:1, :]
    for k in range(GROUPS):
        turned_ref[:, blk(k)] = student_ref[blk(k), :].astype(f32).T.astype(bf16)
    hits = jnp.zeros((LANE, LANE), f32)
    number = lax.broadcasted_iota(jnp.int32, (LANE, LANE), 0).astype(f32)
    for k in range(GROUPS):
        hits = hits + jnp.where(number == lang_ref[k : k + 1, :], 1.0, 0.0)
    count_ref[...] = jnp.broadcast_to(row_totals(hits), (8, LANE))
    acc_ref[...] = jnp.zeros((ROWS, LANE), f32)
    exp_ref[...] = jnp.zeros((ROWS, LANE), f32)

    def step(chunk, _):
        cols = chunk_cols(chunk)
        unit = unit_ref[:, cols]
        d_ref[...] = jnp.dot(teacher_ref[...], unit, preferred_element_type=f32)
        l_ref[...] = jnp.dot(student_ref[...], unit, preferred_element_type=f32)
        for k in range(GROUPS):
            e = jnp.exp(d_ref[blk(k), :] * teacher_scale)
            e_ref[blk(k), cols] = e
            acc_ref[blk(k), :] += lane_sum(e)
            exp_ref[blk(k), :] += lane_sum(jnp.exp(l_ref[blk(k), :] * student_scale))
        return 0

    lax.fori_loop(0, COLS // CHUNK, step, 0)
    send_rows(msg_ref, all_row_totals(acc_ref), all_row_totals(exp_ref))


def send_rows(msg_ref, *parts):
    for peer in range(PEERS):
        for n, part in enumerate(parts):
            msg_ref[peer, 8 * n : 8 * n + 8, :] = part


def peer_sum(recv_ref, low, high):
    total = recv_ref[0, low:high, :].astype(f32)
    for peer in range(1, recv_ref.shape[0]):
        total = total + recv_ref[peer, low:high, :].astype(f32)
    return total


def column_pass(recv_ref, e_ref, count_ref, msg_ref, acc_ref):
    row_weight = 1.0 / peer_sum(recv_ref, 0, 8)
    for k in range(GROUPS):
        factor = lanes(row_weight[k : k + 1, :])
        for j in range(COLS // LANE):
            part = jnp.sum((e_ref[blk(k), blk(j)] * factor).reshape(LANE // 8, 8, LANE), axis=0)
            acc_ref[j] = part if k == 0 else acc_ref[j] + part
    sums = jnp.concatenate([jnp.sum(acc_ref[j], axis=0, keepdims=True) for j in range(COLS // LANE)], axis=0)
    for peer in range(Z):
        msg_ref[peer, 0:16, :] = sums
        if msg_ref.shape[1] > 16:
            msg_ref[peer, 16:24, :] = count_ref[...]


def weighted_rows(e_ref, col_weight):
    out = []
    for k in range(GROUPS):
        acc = e_ref[blk(k), blk(0)] * col_weight[0:1, :]
        for j in range(1, COLS // LANE):
            acc = acc + e_ref[blk(k), blk(j)] * col_weight[j : j + 1, :]
        out.append(row_totals(acc))
    return jnp.concatenate(out, axis=0)


def row_pass(recv_ref, e_ref, msg_ref, count_ref):
    if recv_ref.shape[1] > 16:
        count_ref[...] = peer_sum(recv_ref, 16, 24)
    else:
        count_ref[...] = jnp.zeros((8, LANE), f32)
    send_rows(msg_ref, weighted_rows(e_ref, 1.0 / peer_sum(recv_ref, 0, 16)))


def row_last(recv_ref, e_ref, student_ref, unit_ref, msg_ref, col_ref, acc_ref, dot_ref, d_ref):
    col_ref[...] = 1.0 / peer_sum(recv_ref, 0, 16)
    acc_ref[...] = jnp.zeros((ROWS, LANE), f32)
    dot_ref[...] = jnp.zeros((ROWS, LANE), f32)

    def step(chunk, _):
        d_ref[...] = jnp.dot(student_ref[...], unit_ref[:, chunk_cols(chunk)], preferred_element_type=f32)
        weight = [col_ref[pl.ds(chunk * PARTS + part, 1), :] for part in range(PARTS)]
        for k in range(GROUPS):
            total, dot = acc_ref[blk(k), :], dot_ref[blk(k), :]
            for part in range(PARTS):
                here = pl.ds(pl.multiple_of(chunk * CHUNK + part * LANE, LANE), LANE)
                t = e_ref[blk(k), here] * weight[part]
                total = total + t
                dot = dot + t * d_ref[blk(k), blk(part)]
            acc_ref[blk(k), :] = total
            dot_ref[blk(k), :] = dot
        return 0

    lax.fori_loop(0, COLS // CHUNK, step, 0)
    send_rows(msg_ref, all_row_totals(acc_ref), all_row_totals(dot_ref) * student_scale)


def gradients(
    last_ref, first_ref, lang_ref, count_ref, e_ref, col_ref, student_ref, turned_ref, unit_ref, w_ref, inv_ref,
    out_hbm, own_ref, send_ref, a_ref, b_ref, d_ref, g_ref, out_ref, u_ref, sems,
):
    row_sum = peer_sum(last_ref, 0, 8)
    dot_sum = peer_sum(last_ref, 8, 16)
    exp_sum = peer_sum(first_ref, 8, 16)
    row_weight = 1.0 / row_sum
    target_sum = row_weight * row_sum
    cross = jnp.log(exp_sum) * target_sum - row_weight * dot_sum

    counts = count_ref[0:1, :]
    present = jnp.sum(jnp.where(counts > 0.5, 1.0, 0.0), axis=1, keepdims=True)
    count_rows = lanes(counts)
    number = lax.broadcasted_iota(jnp.int32, (LANE, LANE), 0).astype(f32)
    own = [
        jnp.sum(jnp.where(number == lang_ref[k : k + 1, :], count_rows, 0.0), axis=0, keepdims=True)
        for k in range(GROUPS)
    ]
    token_weight = 1.0 / (jnp.concatenate(own, axis=0) * present)
    loss = jnp.sum(jnp.sum(token_weight * cross, axis=1, keepdims=True), axis=0, keepdims=True)
    soft_factor = grad_scale * token_weight * target_sum / exp_sum
    target_factor = grad_scale * token_weight * row_weight
    for k in range(GROUPS):
        a_ref[blk(k), :] = lanes(soft_factor[k : k + 1, :])
        b_ref[blk(k), :] = lanes(target_factor[k : k + 1, :])

    def send(chunk, width):
        cols = pl.ds(pl.multiple_of(chunk * CHUNK, CHUNK), width)
        return pltpu.make_async_copy(out_ref.at[:, cols], out_hbm.at[:, cols], sems.at[chunk])

    loss_high, _ = split(loss)
    loss_mid, loss_low = split(loss - loss_high.astype(f32))
    lane = lax.broadcasted_iota(jnp.int32, (FEAT, LANE), 1)
    packed = jnp.where(lane == 0, loss_high.astype(f32), jnp.where(lane == 1, loss_mid.astype(f32), loss_low.astype(f32)))
    out_ref[:, COLS : COLS + LANE] = packed.astype(bf16)
    send(COLS // CHUNK, LOSS_LANES).start()

    u_ref[...] = jnp.zeros((ROWS, FEAT), f32)

    def step(chunk, _):
        cols = chunk_cols(chunk)
        unit = unit_ref[:, cols]
        d_ref[...] = jnp.dot(student_ref[...], unit, preferred_element_type=f32)
        weight = [col_ref[pl.ds(chunk * PARTS + part, 1), :] for part in range(PARTS)]
        for k in range(GROUPS):
            a, b = a_ref[blk(k), :], b_ref[blk(k), :]
            for part in range(PARTS):
                here = pl.ds(pl.multiple_of(chunk * CHUNK + part * LANE, LANE), LANE)
                soft = a * jnp.exp(d_ref[blk(k), blk(part)] * student_scale)
                target = b * e_ref[blk(k), here] * weight[part]
                g_ref[blk(k), blk(part)] = (soft - target).astype(bf16)
        full = jnp.dot(turned_ref[...], g_ref[...], preferred_element_type=f32) * student_scale
        w = w_ref[:, cols].astype(f32)
        inv = inv_ref[:, cols]
        inner = jnp.sum(w * full, axis=0, keepdims=True)
        out_ref[:, cols] = (inv * full - w * (inv * inv * inv * inner)).astype(bf16)
        send(chunk, CHUNK).start()
        u_ref[...] += nt(g_ref[...], unit)
        return 0

    lax.fori_loop(0, COLS // CHUNK, step, 0)
    core = lax.axis_index("c")
    for x in range(X):
        for ref, c in ((own_ref, core), (send_ref, 1 - core)):
            ref[x] = u_ref[pl.ds(pl.multiple_of((x * C + c) * TOK, TOK), TOK), :]
    for chunk in range(COLS // CHUNK):
        send(chunk, CHUNK).wait()
    send(COLS // CHUNK, LOSS_LANES).wait()


def add_core(own_ref, other_ref, mine_ref, one_ref, two_ref, three_ref):
    here = lax.axis_index("x")
    for shift, ref in enumerate((mine_ref, one_ref, two_ref, three_ref)):
        x = lax.rem(here + shift, X)
        ref[...] = (own_ref[x] + other_ref[x]).astype(ref.dtype)


def add_x(mine_ref, one_ref, two_ref, three_ref, out_ref):
    out_ref[...] = mine_ref[...] + one_ref[...].astype(f32) + two_ref[...].astype(f32) + three_ref[...].astype(f32)


def scatter_rows(pos_hbm, rows_ref, own_ref, one_ref, two_ref, three_ref, out_ref, all_ref, pos_ref, sems):
    fetch((pos_hbm,), (pos_ref,), sems)
    y = lax.axis_index("y")
    for shift, ref in enumerate((own_ref, one_ref, two_ref, three_ref)):
        all_ref[lax.rem(y - shift + Y, Y)] = ref[...]
    grad_unit = all_ref[0]
    for other in range(1, Y):
        grad_unit = grad_unit + all_ref[other]
    grad_unit = grad_unit * student_scale
    rows = rows_ref[...]
    row_inv = unit_inverse(rows)
    along = jnp.sum(rows * grad_unit, axis=1, keepdims=True)
    grad_rows = row_inv * grad_unit - rows * (row_inv * row_inv * row_inv) * along
    where = lax.broadcasted_iota(jnp.int32, (FEAT, TOK), 0) == pos_ref[...]
    picker = jnp.where(where, 1.0, 0.0).astype(bf16)
    high, _ = split(grad_rows)
    mid, low = split(grad_rows - high.astype(f32))
    out_ref[...] = (
        jnp.dot(picker, high, preferred_element_type=f32)
        + jnp.dot(picker, mid, preferred_element_type=f32)
        + jnp.dot(picker, low, preferred_element_type=f32)
    )


def add_groups(recv_ref, own_ref, other_ref, loss_ref):
    first = lax.axis_index("c") == 0
    for x in range(X):
        for chunk in range(COLS // CHUNK):
            cols = pl.ds(chunk * CHUNK, CHUNK)
            total = recv_ref[x, :, cols].astype(f32)
            for z in range(1, Z):
                total = total + recv_ref[z * X + x, :, cols].astype(f32)
            there = pl.ds(x * COLS + chunk * CHUNK, CHUNK)
            own_ref[:, there] = jnp.where(first, total[0:4], total[4:8])
            other_ref[:, there] = jnp.where(first, total[4:8], total[0:4])
    loss = recv_ref[0, :, COLS : COLS + LANE].astype(f32)
    for z in range(1, Z):
        loss = loss + recv_ref[z * X, :, COLS : COLS + LANE].astype(f32)
    lane = lax.broadcasted_iota(jnp.int32, loss.shape, 1)
    loss_ref[...] = jnp.sum(jnp.where(lane < 3, loss, 0.0)[0:1, :], axis=1, keepdims=True)


def join(own_ref, other_ref, out_ref):
    core = lax.axis_index("c")
    for x in range(X):
        for ref, c in ((own_ref, core), (other_ref, 1 - core)):
            there = pl.ds(pl.multiple_of((x * C + c) * COLS, COLS), COLS)
            out_ref[:, there] = ref[:, x * COLS : (x + 1) * COLS]


def exchange(message, axes):
    return lax.all_to_all(message, axes, 0, 0)


def other_core(values):
    return lax.ppermute(values, "c", [(0, 1), (1, 0)])


def shifted(values, axis, size, shift):
    return lax.ppermute(values, axis, [(i, (i + shift) % size) for i in range(size)])


def local(teacher_seq, student_seq, prototypes, positions, languages):
    shape = jax.ShapeDtypeStruct
    kept = pltpu.VMEM
    sems = pltpu.SemaphoreType.DMA
    z_axis, row_axes = ("z",), ("x", "c", "y")
    pos = positions[None, :]

    units, rows = call(
        pick_rows,
        (shape((X, TOK + 16, 2 * FEAT), bf16), shape((TOK, FEAT), f32)),
        [
            pltpu.VMEM((1, TOK), jnp.int32),
            pltpu.VMEM((1, TOK), jnp.int32),
            pltpu.VMEM((FEAT, FEAT), bf16),
            pltpu.VMEM((FEAT, FEAT), bf16),
            sems((4,)),
        ],
        anywhere=(0, 1, 2, 3),
    )(pos, languages[None, :], teacher_seq, student_seq)
    w, unit, inv = call(
        weights,
        (shape((FEAT, COLS), bf16), shape((FEAT, COLS), bf16), shape((1, COLS), f32)),
        [sems((1,))],
        anywhere=(0,),
    )(prototypes)
    totals = pltpu.VMEM((ROWS, LANE), f32)
    products = pltpu.VMEM((ROWS, CHUNK), f32)
    units = exchange(units, ("x",))
    e, student, turned, lang, count, message = call(
        start,
        (
            kept((ROWS, COLS), f32),
            shape((ROWS, FEAT), bf16),
            shape((FEAT, ROWS), bf16),
            shape((8, LANE), f32),
            shape((8, LANE), f32),
            shape((PEERS, 16, LANE), f32),
        ),
        [pltpu.VMEM((ROWS, FEAT), bf16), totals, totals, products, products],
    )(units, other_core(units), unit)

    for sweep in range(ITERS):
        received = exchange(message, row_axes)
        if sweep == 0:
            first = received
        out = shape((Z, 24 if sweep == 0 else 16, LANE), f32)
        message = call(column_pass, out, [pltpu.VMEM((COLS // LANE, 8, LANE), f32)])(received, e, count)
        columns = exchange(message, z_axis)
        if sweep < ITERS - 1:
            message, summed = call(row_pass, (shape((PEERS, 8, LANE), f32), shape((8, LANE), f32)))(columns, e)
            counts = summed if sweep == 0 else counts
        else:
            message, col = call(
                row_last, (shape((PEERS, 16, LANE), f32), shape((16, LANE), f32)), [totals, totals, products]
            )(columns, e, student, unit)
    last = exchange(message, row_axes)
    grad, own, send = call(
        gradients,
        (pltpu.HBM((FEAT, COLS + LOSS_LANES), bf16), shape((X, TOK, FEAT), f32), shape((X, TOK, FEAT), f32)),
        [
            totals,
            totals,
            products,
            pltpu.VMEM((ROWS, CHUNK), bf16),
            pltpu.VMEM((FEAT, COLS + LOSS_LANES), bf16),
            pltpu.VMEM((ROWS, FEAT), f32),
            sems((COLS // CHUNK + 1,)),
        ],
        out_anywhere=(0,),
    )(last, first, lang, counts, e, col, student, turned, unit, w, inv)
    block = shape((TOK, FEAT), f32)
    short = shape((TOK, FEAT), bf16)
    mine, *parts = call(add_core, (block, short, short, short))(own, other_core(send))
    mine = call(add_x, block)(mine, *(shifted(part, "x", X, s) for s, part in enumerate(parts, 1)))
    others = [shifted(mine, "y", Y, s) for s in range(1, Y)]
    grad = exchange(grad.reshape(Z * X, 8, COLS + LOSS_LANES), ("z", "x"))
    grad_student = call(
        scatter_rows,
        shape((FEAT, FEAT), f32),
        [pltpu.VMEM((Y, TOK, FEAT), f32), pltpu.VMEM((1, TOK), jnp.int32), sems((1,))],
        anywhere=(0,),
    )(pos, rows, mine, *others)
    grad, grad_student = lax.optimization_barrier((grad, grad_student))
    half = shape((4, X * COLS), f32)
    mine, theirs, loss = call(add_groups, (half, half, shape((1, 1), f32)))(grad)
    grad_prototypes = call(join, shape((4, GROUPS * COLS), f32))(mine, other_core(theirs))
    return (loss[0, 0], grad_student, grad_prototypes)


def solution(mesh):
    fine = Mesh(mesh.devices.reshape(Z, X, C, Y), ("z", "x", "c", "y"))
    tok = ("z", "x", "c")
    in_specs = (P(tok, None), P(tok, None), P(None, "y"), P(tok), P(tok))
    out_specs = (P(), P(tok, None), P(tok, "y"))
    return jax.shard_map(local, mesh=fine, in_specs=in_specs, out_specs=out_specs, check_vma=False)
```

```python
import jax
import jax.numpy as jnp
from jax import lax
from jax.experimental import pallas as pl
from jax.experimental.pallas import tpu as pltpu
from jax.sharding import Mesh, PartitionSpec as P

LANGS = 100
ITERS = 3

epsilon = 1e-06
teacher_scale = 20.0
student_scale = 10.0
grad_scale = 8388608.0

Z, X, C, Y = 8, 4, 2, 4
TOK = 128
GROUPS = X * C
ROWS = GROUPS * TOK
COLS = 2048
FEAT = 256
LANE = 128
CHUNK = 512
PARTS = CHUNK // LANE
PEERS = X * C * Y
LOSS_LANES = 128
f32 = jnp.float32
bf16 = jnp.bfloat16


def call(kernel, out_shape, scratch=(), anywhere=(), out_anywhere=(), mib=24):
    def run(*args):
        space = lambda far: pl.BlockSpec(memory_space=pltpu.HBM if far else pltpu.VMEM)
        args = [pltpu.with_memory_space_constraint(a, pltpu.HBM) if i in anywhere else a for i, a in enumerate(args)]
        multiple = isinstance(out_shape, (tuple, list))
        outs = [space(i in out_anywhere) for i in range(len(out_shape) if multiple else 1)]
        return pl.pallas_call(
            kernel,
            out_shape=out_shape,
            in_specs=[space(i in anywhere) for i in range(len(args))],
            out_specs=outs if multiple else outs[0],
            scratch_shapes=list(scratch),
            compiler_params=pltpu.CompilerParams(vmem_limit_bytes=mib << 20),
            name=kernel.__name__,
        )(*args)

    return run


def lanes(row):
    return jnp.broadcast_to(row, (LANE, LANE)).T


def row_totals(block):
    return jnp.sum(block.T, axis=0, keepdims=True)


def blk(index):
    return pl.ds(index * LANE, LANE)


def split(values):
    high = values.astype(bf16)
    return high, (values - high.astype(f32)).astype(bf16)


def nt(left, right):
    return lax.dot_general(left, right, (((1,), (1,)), ((), ())), preferred_element_type=f32)


def tn(left, right):
    return lax.dot_general(left, right, (((0,), (0,)), ((), ())), preferred_element_type=f32)


def unit_inverse(values):
    return lax.rsqrt(jnp.sum(values * values, axis=1, keepdims=True) + epsilon)


def fetch(sources, targets, sems):
    copies = [pltpu.make_async_copy(a, b, sems.at[n]) for n, (a, b) in enumerate(zip(sources, targets))]
    for copy in copies:
        copy.start()
    for copy in copies:
        copy.wait()


def pick_rows(pos_hbm, lang_hbm, teacher_hbm, student_hbm, out_ref, rows_ref, pos_ref, lang_ref, teacher_ref, student_ref, sems):
    fetch((pos_hbm, lang_hbm, teacher_hbm, student_hbm), (pos_ref, lang_ref, teacher_ref, student_ref), sems)
    where = lax.broadcasted_iota(jnp.int32, (FEAT, TOK), 0) == pos_ref[...]
    picker = jnp.where(where, 1.0, 0.0).astype(bf16)
    teacher = tn(picker, teacher_ref[...])
    student = tn(picker, student_ref[...])
    teacher_unit = (teacher * unit_inverse(teacher)).astype(bf16)
    student_unit = (student * unit_inverse(student)).astype(bf16)
    language = jnp.broadcast_to(lang_ref[...].astype(f32), (16, TOK)).astype(bf16)
    rows_ref[...] = student
    for peer in range(X):
        out_ref[peer, 0:TOK, 0:FEAT] = teacher_unit
        out_ref[peer, 0:TOK, FEAT : 2 * FEAT] = student_unit
        for part in range(4):
            out_ref[peer, TOK : TOK + 16, part * LANE : (part + 1) * LANE] = language


def weights(proto_hbm, w_ref, unit_ref, inv_ref, sems):
    group = lax.axis_index("x") * C + lax.axis_index("c")
    here = pl.ds(pl.multiple_of(group * COLS, COLS), COLS)
    fetch((proto_hbm.at[:, here],), (w_ref,), sems)
    for chunk in range(COLS // CHUNK):
        cols = pl.ds(chunk * CHUNK, CHUNK)
        w = w_ref[:, cols].astype(f32)
        inv = lax.rsqrt(jnp.sum(w * w, axis=0, keepdims=True) + epsilon)
        inv_ref[:, cols] = inv
        unit_ref[:, cols] = (w * inv).astype(bf16)


def lane_sum(block):
    total = block[:, 0:LANE]
    for part in range(1, PARTS):
        total = total + block[:, part * LANE : (part + 1) * LANE]
    return total


def all_row_totals(acc_ref):
    return jnp.concatenate([row_totals(acc_ref[blk(k), :]) for k in range(GROUPS)], axis=0)


def start(
    own_ref, other_ref, unit_ref, e_ref, logit_ref, turned_ref, lang_ref, count_ref, msg_ref,
    teacher_ref, student_ref, acc_ref, exp_ref, d_ref,
):
    core = lax.axis_index("c")
    for x in range(X):
        for ref, c in ((own_ref, core), (other_ref, 1 - core)):
            here = pl.ds(pl.multiple_of((x * C + c) * TOK, TOK), TOK)
            teacher_ref[here, :] = ref[x, 0:TOK, 0:FEAT]
            student_ref[here, :] = ref[x, 0:TOK, FEAT : 2 * FEAT]
            lang_ref[pl.ds(x * C + c, 1), :] = ref[x, TOK : TOK + 16, 0:LANE].astype(f32)[0:1, :]
    for k in range(GROUPS):
        turned_ref[:, blk(k)] = student_ref[blk(k), :].astype(f32).T.astype(bf16)
    hits = jnp.zeros((LANE, LANE), f32)
    number = lax.broadcasted_iota(jnp.int32, (LANE, LANE), 0).astype(f32)
    for k in range(GROUPS):
        hits = hits + jnp.where(number == lang_ref[k : k + 1, :], 1.0, 0.0)
    count_ref[...] = jnp.broadcast_to(row_totals(hits), (8, LANE))
    acc_ref[...] = jnp.zeros((ROWS, LANE), f32)
    exp_ref[...] = jnp.zeros((ROWS, LANE), f32)

    def step(chunk):
        cols = pl.ds(chunk * CHUNK, CHUNK)
        unit = unit_ref[:, cols]
        d_ref[...] = jnp.dot(teacher_ref[...], unit, preferred_element_type=f32)
        logit_ref[:, cols] = jnp.dot(student_ref[...], unit, preferred_element_type=f32)
        for k in range(GROUPS):
            e = jnp.exp(d_ref[blk(k), :] * teacher_scale)
            e_ref[blk(k), cols] = e
            acc_ref[blk(k), :] += lane_sum(e)
            exp_ref[blk(k), :] += lane_sum(jnp.exp(logit_ref[blk(k), cols] * student_scale))

    for chunk in range(COLS // CHUNK):
        step(chunk)
    send_rows(msg_ref, all_row_totals(acc_ref), all_row_totals(exp_ref))


def send_rows(msg_ref, *parts):
    for peer in range(PEERS):
        for n, part in enumerate(parts):
            msg_ref[peer, 8 * n : 8 * n + 8, :] = part


def peer_sum(recv_ref, low, high):
    total = recv_ref[0, low:high, :].astype(f32)
    for peer in range(1, recv_ref.shape[0]):
        total = total + recv_ref[peer, low:high, :].astype(f32)
    return total


def column_pass(recv_ref, e_ref, count_ref, msg_ref, acc_ref):
    row_weight = 1.0 / peer_sum(recv_ref, 0, 8)
    for k in range(GROUPS):
        factor = lanes(row_weight[k : k + 1, :])
        for j in range(COLS // LANE):
            part = jnp.sum((e_ref[blk(k), blk(j)] * factor).reshape(LANE // 8, 8, LANE), axis=0)
            acc_ref[j] = part if k == 0 else acc_ref[j] + part
    sums = jnp.concatenate([jnp.sum(acc_ref[j], axis=0, keepdims=True) for j in range(COLS // LANE)], axis=0)
    for peer in range(Z):
        msg_ref[peer, 0:16, :] = sums
        if msg_ref.shape[1] > 16:
            msg_ref[peer, 16:24, :] = count_ref[...]


def weighted_rows(e_ref, col_weight):
    out = []
    for k in range(GROUPS):
        acc = e_ref[blk(k), blk(0)] * col_weight[0:1, :]
        for j in range(1, COLS // LANE):
            acc = acc + e_ref[blk(k), blk(j)] * col_weight[j : j + 1, :]
        out.append(row_totals(acc))
    return jnp.concatenate(out, axis=0)


def row_pass(recv_ref, e_ref, msg_ref, *count_ref):
    for ref in count_ref:
        ref[...] = peer_sum(recv_ref, 16, 24)
    send_rows(msg_ref, weighted_rows(e_ref, 1.0 / peer_sum(recv_ref, 0, 16)))


def row_last(recv_ref, e_ref, logit_ref, msg_ref, col_ref):
    col_weight = 1.0 / peer_sum(recv_ref, 0, 16)
    col_ref[...] = col_weight
    sums, dots = [], []
    for k in range(GROUPS):
        total = e_ref[blk(k), blk(0)] * col_weight[0:1, :]
        dot = total * logit_ref[blk(k), blk(0)]
        for j in range(1, COLS // LANE):
            t = e_ref[blk(k), blk(j)] * col_weight[j : j + 1, :]
            total = total + t
            dot = dot + t * logit_ref[blk(k), blk(j)]
        sums.append(row_totals(total))
        dots.append(row_totals(dot) * student_scale)
    send_rows(msg_ref, jnp.concatenate(sums, axis=0), jnp.concatenate(dots, axis=0))


def gradients(
    last_ref, first_ref, lang_ref, count_ref, e_ref, logit_ref, col_ref, turned_ref, unit_ref, w_ref, inv_ref,
    out_hbm, own_ref, send_ref, a_ref, b_ref, g_ref, out_ref, u_ref, sems,
):
    row_sum = peer_sum(last_ref, 0, 8)
    dot_sum = peer_sum(last_ref, 8, 16)
    exp_sum = peer_sum(first_ref, 8, 16)
    row_weight = 1.0 / row_sum
    target_sum = row_weight * row_sum
    cross = jnp.log(exp_sum) * target_sum - row_weight * dot_sum

    counts = count_ref[0:1, :]
    present = jnp.sum(jnp.where(counts > 0.5, 1.0, 0.0), axis=1, keepdims=True)
    count_rows = lanes(counts)
    number = lax.broadcasted_iota(jnp.int32, (LANE, LANE), 0).astype(f32)
    own = [
        jnp.sum(jnp.where(number == lang_ref[k : k + 1, :], count_rows, 0.0), axis=0, keepdims=True)
        for k in range(GROUPS)
    ]
    token_weight = 1.0 / (jnp.concatenate(own, axis=0) * present)
    loss = jnp.sum(jnp.sum(token_weight * cross, axis=1, keepdims=True), axis=0, keepdims=True)
    soft_factor = grad_scale * token_weight * target_sum / exp_sum
    target_factor = grad_scale * token_weight * row_weight
    for k in range(GROUPS):
        a_ref[blk(k), :] = lanes(soft_factor[k : k + 1, :])
        b_ref[blk(k), :] = lanes(target_factor[k : k + 1, :])

    def send(chunk, width):
        cols = pl.ds(pl.multiple_of(chunk * CHUNK, CHUNK), width)
        return pltpu.make_async_copy(out_ref.at[:, cols], out_hbm.at[:, cols], sems.at[chunk])

    loss_high, _ = split(loss)
    loss_mid, loss_low = split(loss - loss_high.astype(f32))
    lane = lax.broadcasted_iota(jnp.int32, (FEAT, LANE), 1)
    packed = jnp.where(lane == 0, loss_high.astype(f32), jnp.where(lane == 1, loss_mid.astype(f32), loss_low.astype(f32)))
    out_ref[:, COLS : COLS + LANE] = packed.astype(bf16)
    send(COLS // CHUNK, LOSS_LANES).start()

    for chunk in range(COLS // CHUNK):
        cols = pl.ds(chunk * CHUNK, CHUNK)
        for k in range(GROUPS):
            a, b = a_ref[blk(k), :], b_ref[blk(k), :]
            for part in range(PARTS):
                j = chunk * PARTS + part
                soft = a * jnp.exp(logit_ref[blk(k), blk(j)] * student_scale)
                target = b * e_ref[blk(k), blk(j)] * col_ref[j : j + 1, :]
                g_ref[blk(k), blk(j)] = (soft - target).astype(bf16)
        full = jnp.dot(turned_ref[...], g_ref[:, cols], preferred_element_type=f32) * student_scale
        w = w_ref[:, cols].astype(f32)
        inv = inv_ref[:, cols]
        inner = jnp.sum(w * full, axis=0, keepdims=True)
        out_ref[:, cols] = (inv * full - w * (inv * inv * inv * inner)).astype(bf16)
        send(chunk, CHUNK).start()
    u_ref[...] = nt(g_ref[...], unit_ref[...])
    core = lax.axis_index("c")
    for x in range(X):
        for ref, c in ((own_ref, core), (send_ref, 1 - core)):
            ref[x] = u_ref[pl.ds(pl.multiple_of((x * C + c) * TOK, TOK), TOK), :]
    for chunk in range(COLS // CHUNK):
        send(chunk, CHUNK).wait()
    send(COLS // CHUNK, LOSS_LANES).wait()


def add_core(own_ref, other_ref, mine_ref, one_ref, two_ref, three_ref):
    here = lax.axis_index("x")
    for shift, ref in enumerate((mine_ref, one_ref, two_ref, three_ref)):
        x = lax.rem(here + shift, X)
        ref[...] = (own_ref[x] + other_ref[x]).astype(ref.dtype)


def add_x(mine_ref, one_ref, two_ref, three_ref, out_ref):
    out_ref[...] = mine_ref[...] + one_ref[...].astype(f32) + two_ref[...].astype(f32) + three_ref[...].astype(f32)


def scatter_rows(pos_hbm, rows_ref, own_ref, one_ref, two_ref, three_ref, out_ref, all_ref, pos_ref, sems):
    fetch((pos_hbm,), (pos_ref,), sems)
    y = lax.axis_index("y")
    for shift, ref in enumerate((own_ref, one_ref, two_ref, three_ref)):
        all_ref[lax.rem(y - shift + Y, Y)] = ref[...]
    grad_unit = all_ref[0]
    for other in range(1, Y):
        grad_unit = grad_unit + all_ref[other]
    grad_unit = grad_unit * student_scale
    rows = rows_ref[...]
    row_inv = unit_inverse(rows)
    along = jnp.sum(rows * grad_unit, axis=1, keepdims=True)
    grad_rows = row_inv * grad_unit - rows * (row_inv * row_inv * row_inv) * along
    where = lax.broadcasted_iota(jnp.int32, (FEAT, TOK), 0) == pos_ref[...]
    picker = jnp.where(where, 1.0, 0.0).astype(bf16)
    high, _ = split(grad_rows)
    mid, low = split(grad_rows - high.astype(f32))
    out_ref[...] = (
        jnp.dot(picker, high, preferred_element_type=f32)
        + jnp.dot(picker, mid, preferred_element_type=f32)
        + jnp.dot(picker, low, preferred_element_type=f32)
    )


def add_groups(recv_ref, own_ref, other_ref, loss_ref):
    first = lax.axis_index("c") == 0
    for x in range(X):
        for chunk in range(COLS // CHUNK):
            cols = pl.ds(chunk * CHUNK, CHUNK)
            total = recv_ref[x, :, cols].astype(f32)
            for z in range(1, Z):
                total = total + recv_ref[z * X + x, :, cols].astype(f32)
            there = pl.ds(x * COLS + chunk * CHUNK, CHUNK)
            own_ref[:, there] = jnp.where(first, total[0:4], total[4:8])
            other_ref[:, there] = jnp.where(first, total[4:8], total[0:4])
    loss = recv_ref[0, :, COLS : COLS + LANE].astype(f32)
    for z in range(1, Z):
        loss = loss + recv_ref[z * X, :, COLS : COLS + LANE].astype(f32)
    lane = lax.broadcasted_iota(jnp.int32, loss.shape, 1)
    loss_ref[...] = jnp.sum(jnp.where(lane < 3, loss, 0.0)[0:1, :], axis=1, keepdims=True)


def join(own_ref, other_ref, out_ref):
    core = lax.axis_index("c")
    for x in range(X):
        for ref, c in ((own_ref, core), (other_ref, 1 - core)):
            there = pl.ds(pl.multiple_of((x * C + c) * COLS, COLS), COLS)
            out_ref[:, there] = ref[:, x * COLS : (x + 1) * COLS]


def exchange(message, axes):
    return lax.all_to_all(message, axes, 0, 0)


def other_core(values):
    return lax.ppermute(values, "c", [(0, 1), (1, 0)])


def shifted(values, axis, size, shift):
    return lax.ppermute(values, axis, [(i, (i + shift) % size) for i in range(size)])


def local(teacher_seq, student_seq, prototypes, positions, languages):
    shape = jax.ShapeDtypeStruct
    kept = pltpu.VMEM
    sems = pltpu.SemaphoreType.DMA
    z_axis, row_axes = ("z",), ("x", "c", "y")
    pos = positions[None, :]

    units, rows = call(
        pick_rows,
        (shape((X, TOK + 16, 2 * FEAT), bf16), shape((TOK, FEAT), f32)),
        [
            pltpu.VMEM((1, TOK), jnp.int32),
            pltpu.VMEM((1, TOK), jnp.int32),
            pltpu.VMEM((FEAT, FEAT), bf16),
            pltpu.VMEM((FEAT, FEAT), bf16),
            sems((4,)),
        ],
        anywhere=(0, 1, 2, 3),
    )(pos, languages[None, :], teacher_seq, student_seq)
    w, unit, inv = call(
        weights,
        (shape((FEAT, COLS), bf16), shape((FEAT, COLS), bf16), shape((1, COLS), f32)),
        [sems((1,))],
        anywhere=(0,),
    )(prototypes)
    totals = pltpu.VMEM((ROWS, LANE), f32)
    products = pltpu.VMEM((ROWS, CHUNK), f32)
    units = exchange(units, ("x",))
    e, logits, turned, lang, count, message = call(
        start,
        (
            kept((ROWS, COLS), f32),
            kept((ROWS, COLS), f32),
            shape((FEAT, ROWS), bf16),
            shape((8, LANE), f32),
            shape((8, LANE), f32),
            shape((PEERS, 16, LANE), f32),
        ),
        [pltpu.VMEM((ROWS, FEAT), bf16), pltpu.VMEM((ROWS, FEAT), bf16), totals, totals, products],
    )(units, other_core(units), unit)

    for sweep in range(ITERS):
        received = exchange(message, row_axes)
        if sweep == 0:
            first = received
        out = shape((Z, 24 if sweep == 0 else 16, LANE), f32)
        message = call(column_pass, out, [pltpu.VMEM((COLS // LANE, 8, LANE), f32)])(received, e, count)
        columns = exchange(message, z_axis)
        if sweep < ITERS - 1:
            small = shape((8, LANE), f32)
            message, *summed = call(row_pass, (shape((PEERS, 8, LANE), f32),) + (small,) * (sweep == 0))(columns, e)
            counts = summed[0] if sweep == 0 else counts
        else:
            message, col = call(row_last, (shape((PEERS, 16, LANE), f32), shape((16, LANE), f32)))(columns, e, logits)
    last = exchange(message, row_axes)
    grad, own, send = call(
        gradients,
        (pltpu.HBM((FEAT, COLS + LOSS_LANES), bf16), shape((X, TOK, FEAT), f32), shape((X, TOK, FEAT), f32)),
        [
            totals,
            totals,
            pltpu.VMEM((ROWS, COLS), bf16),
            pltpu.VMEM((FEAT, COLS + LOSS_LANES), bf16),
            pltpu.VMEM((ROWS, FEAT), f32),
            sems((COLS // CHUNK + 1,)),
        ],
        out_anywhere=(0,),
    )(last, first, lang, counts, e, logits, col, turned, unit, w, inv)
    block = shape((TOK, FEAT), f32)
    short = shape((TOK, FEAT), bf16)
    mine, *parts = call(add_core, (block, short, short, short))(own, other_core(send))
    mine = call(add_x, block)(mine, *(shifted(part, "x", X, s) for s, part in enumerate(parts, 1)))
    others = [shifted(mine, "y", Y, s) for s in range(1, Y)]
    grad = exchange(grad.reshape(Z * X, 8, COLS + LOSS_LANES), ("z", "x"))
    grad_student = call(
        scatter_rows,
        shape((FEAT, FEAT), f32),
        [pltpu.VMEM((Y, TOK, FEAT), f32), pltpu.VMEM((1, TOK), jnp.int32), sems((1,))],
        anywhere=(0,),
    )(pos, rows, mine, *others)
    grad, grad_student = lax.optimization_barrier((grad, grad_student))
    half = shape((4, X * COLS), f32)
    mine, theirs, loss = call(add_groups, (half, half, shape((1, 1), f32)))(grad)
    grad_prototypes = call(join, shape((4, GROUPS * COLS), f32))(mine, other_core(theirs))
    return (loss[0, 0], grad_student, grad_prototypes)


def solution(mesh):
    fine = Mesh(mesh.devices.reshape(Z, X, C, Y), ("z", "x", "c", "y"))
    tok = ("z", "x", "c")
    in_specs = (P(tok, None), P(tok, None), P(None, "y"), P(tok), P(tok))
    out_specs = (P(), P(tok, None), P(tok, "y"))
    return jax.shard_map(local, mesh=fine, in_specs=in_specs, out_specs=out_specs, check_vma=False)
```

```python
import jax
import jax.numpy as jnp
from jax import lax
from jax.experimental import pallas as pl
from jax.experimental.pallas import tpu as pltpu
from jax.sharding import Mesh, PartitionSpec as P

LANGS = 100
ITERS = 3

epsilon = 1e-06
teacher_scale = 20.0
student_scale = 10.0
grad_scale = 8388608.0

Z, X, C, Y = 8, 4, 2, 4
TOK = 128
GROUPS = X * C
ROWS = GROUPS * TOK
COLS = 2048
FEAT = 256
LANE = 128
CHUNK = 512
PARTS = CHUNK // LANE
PEERS = X * C * Y
f32 = jnp.float32
bf16 = jnp.bfloat16


def call(kernel, out_shape, scratch=(), anywhere=(), out_anywhere=(), mib=24):
    def run(*args):
        space = lambda far: pl.BlockSpec(memory_space=pltpu.HBM if far else pltpu.VMEM)
        args = [pltpu.with_memory_space_constraint(a, pltpu.HBM) if i in anywhere else a for i, a in enumerate(args)]
        multiple = isinstance(out_shape, (tuple, list))
        outs = [space(i in out_anywhere) for i in range(len(out_shape) if multiple else 1)]
        return pl.pallas_call(
            kernel,
            out_shape=out_shape,
            in_specs=[space(i in anywhere) for i in range(len(args))],
            out_specs=outs if multiple else outs[0],
            scratch_shapes=list(scratch),
            compiler_params=pltpu.CompilerParams(vmem_limit_bytes=mib << 20),
            name=kernel.__name__,
        )(*args)

    return run


def lanes(row):
    return jnp.broadcast_to(row, (LANE, LANE)).T


def row_totals(block):
    return jnp.sum(block.T, axis=0, keepdims=True)


def blk(index):
    return pl.ds(index * LANE, LANE)


def split(values):
    high = values.astype(bf16)
    return high, (values - high.astype(f32)).astype(bf16)


def nt(left, right):
    return lax.dot_general(left, right, (((1,), (1,)), ((), ())), preferred_element_type=f32)


def tn(left, right):
    return lax.dot_general(left, right, (((0,), (0,)), ((), ())), preferred_element_type=f32)


def unit_inverse(values):
    return lax.rsqrt(jnp.sum(values * values, axis=1, keepdims=True) + epsilon)


def fetch(sources, targets, sems):
    copies = [pltpu.make_async_copy(a, b, sems.at[n]) for n, (a, b) in enumerate(zip(sources, targets))]
    for copy in copies:
        copy.start()
    for copy in copies:
        copy.wait()


def pick_rows(pos_hbm, lang_hbm, teacher_hbm, student_hbm, out_ref, rows_ref, pos_ref, lang_ref, teacher_ref, student_ref, sems):
    fetch((pos_hbm, lang_hbm, teacher_hbm, student_hbm), (pos_ref, lang_ref, teacher_ref, student_ref), sems)
    where = lax.broadcasted_iota(jnp.int32, (FEAT, TOK), 0) == pos_ref[...]
    picker = jnp.where(where, 1.0, 0.0).astype(bf16)
    teacher = tn(picker, teacher_ref[...])
    student = tn(picker, student_ref[...])
    teacher_unit = (teacher * unit_inverse(teacher)).astype(bf16)
    student_unit = (student * unit_inverse(student)).astype(bf16)
    language = jnp.broadcast_to(lang_ref[...].astype(f32), (16, TOK)).astype(bf16)
    rows_ref[...] = student
    for peer in range(X):
        out_ref[peer, 0:TOK, 0:FEAT] = teacher_unit
        out_ref[peer, 0:TOK, FEAT : 2 * FEAT] = student_unit
        for part in range(4):
            out_ref[peer, TOK : TOK + 16, part * LANE : (part + 1) * LANE] = language


def weights(proto_hbm, w_ref, unit_ref, inv_ref, sems):
    group = lax.axis_index("x") * C + lax.axis_index("c")
    here = pl.ds(pl.multiple_of(group * COLS, COLS), COLS)
    fetch((proto_hbm.at[:, here],), (w_ref,), sems)
    for chunk in range(COLS // CHUNK):
        cols = pl.ds(chunk * CHUNK, CHUNK)
        w = w_ref[:, cols].astype(f32)
        inv = lax.rsqrt(jnp.sum(w * w, axis=0, keepdims=True) + epsilon)
        inv_ref[:, cols] = inv
        unit_ref[:, cols] = (w * inv).astype(bf16)


def lane_sum(block):
    total = block[:, 0:LANE]
    for part in range(1, PARTS):
        total = total + block[:, part * LANE : (part + 1) * LANE]
    return total


def all_row_totals(acc_ref):
    return jnp.concatenate([row_totals(acc_ref[blk(k), :]) for k in range(GROUPS)], axis=0)


def start(
    own_ref, other_ref, unit_ref, e_ref, logit_ref, turned_ref, lang_ref, count_ref, msg_ref,
    teacher_ref, student_ref, acc_ref, exp_ref, d_ref,
):
    core = lax.axis_index("c")
    for x in range(X):
        for ref, c in ((own_ref, core), (other_ref, 1 - core)):
            here = pl.ds(pl.multiple_of((x * C + c) * TOK, TOK), TOK)
            teacher_ref[here, :] = ref[x, 0:TOK, 0:FEAT]
            student_ref[here, :] = ref[x, 0:TOK, FEAT : 2 * FEAT]
            lang_ref[pl.ds(x * C + c, 1), :] = ref[x, TOK : TOK + 16, 0:LANE].astype(f32)[0:1, :]
    for k in range(GROUPS):
        turned_ref[:, blk(k)] = student_ref[blk(k), :].astype(f32).T.astype(bf16)
    hits = jnp.zeros((LANE, LANE), f32)
    number = lax.broadcasted_iota(jnp.int32, (LANE, LANE), 0).astype(f32)
    for k in range(GROUPS):
        hits = hits + jnp.where(number == lang_ref[k : k + 1, :], 1.0, 0.0)
    count_ref[...] = jnp.broadcast_to(row_totals(hits), (8, LANE))
    acc_ref[...] = jnp.zeros((ROWS, LANE), f32)
    exp_ref[...] = jnp.zeros((ROWS, LANE), f32)

    def step(chunk):
        cols = pl.ds(chunk * CHUNK, CHUNK)
        unit = unit_ref[:, cols]
        d_ref[...] = jnp.dot(teacher_ref[...], unit, preferred_element_type=f32)
        logit_ref[:, cols] = jnp.dot(student_ref[...], unit, preferred_element_type=f32)
        for k in range(GROUPS):
            e = jnp.exp(d_ref[blk(k), :] * teacher_scale)
            e_ref[blk(k), cols] = e
            acc_ref[blk(k), :] += lane_sum(e)
            exp_ref[blk(k), :] += lane_sum(jnp.exp(logit_ref[blk(k), cols] * student_scale))

    for chunk in range(COLS // CHUNK):
        step(chunk)
    send_rows(msg_ref, all_row_totals(acc_ref), all_row_totals(exp_ref))


def send_rows(msg_ref, *parts):
    for peer in range(PEERS):
        for n, part in enumerate(parts):
            msg_ref[peer, 8 * n : 8 * n + 8, :] = part


def peer_sum(recv_ref, low, high):
    total = recv_ref[0, low:high, :].astype(f32)
    for peer in range(1, recv_ref.shape[0]):
        total = total + recv_ref[peer, low:high, :].astype(f32)
    return total


def column_pass(recv_ref, e_ref, count_ref, msg_ref, acc_ref):
    row_weight = 1.0 / peer_sum(recv_ref, 0, 8)
    for k in range(GROUPS):
        factor = lanes(row_weight[k : k + 1, :])
        for j in range(COLS // LANE):
            part = jnp.sum((e_ref[blk(k), blk(j)] * factor).reshape(LANE // 8, 8, LANE), axis=0)
            acc_ref[j] = part if k == 0 else acc_ref[j] + part
    sums = jnp.concatenate([jnp.sum(acc_ref[j], axis=0, keepdims=True) for j in range(COLS // LANE)], axis=0)
    for peer in range(Z):
        msg_ref[peer, 0:16, :] = sums
        if msg_ref.shape[1] > 16:
            msg_ref[peer, 16:24, :] = count_ref[...]


def weighted_rows(e_ref, col_weight):
    out = []
    for k in range(GROUPS):
        acc = e_ref[blk(k), blk(0)] * col_weight[0:1, :]
        for j in range(1, COLS // LANE):
            acc = acc + e_ref[blk(k), blk(j)] * col_weight[j : j + 1, :]
        out.append(row_totals(acc))
    return jnp.concatenate(out, axis=0)


def row_pass(recv_ref, e_ref, msg_ref, *count_ref):
    for ref in count_ref:
        ref[...] = peer_sum(recv_ref, 16, 24)
    send_rows(msg_ref, weighted_rows(e_ref, 1.0 / peer_sum(recv_ref, 0, 16)))


def row_last(recv_ref, e_ref, logit_ref, msg_ref, col_ref):
    col_weight = 1.0 / peer_sum(recv_ref, 0, 16)
    col_ref[...] = col_weight
    sums, dots = [], []
    for k in range(GROUPS):
        total = e_ref[blk(k), blk(0)] * col_weight[0:1, :]
        dot = total * logit_ref[blk(k), blk(0)]
        for j in range(1, COLS // LANE):
            t = e_ref[blk(k), blk(j)] * col_weight[j : j + 1, :]
            total = total + t
            dot = dot + t * logit_ref[blk(k), blk(j)]
        sums.append(row_totals(total))
        dots.append(row_totals(dot) * student_scale)
    send_rows(msg_ref, jnp.concatenate(sums, axis=0), jnp.concatenate(dots, axis=0))


def gradients(
    last_ref, first_ref, lang_ref, count_ref, e_ref, logit_ref, col_ref, turned_ref, unit_ref, w_ref, inv_ref,
    out_hbm, own_ref, send_ref, loss_ref, a_ref, b_ref, g_ref, out_ref, u_ref, sems,
):
    row_sum = peer_sum(last_ref, 0, 8)
    dot_sum = peer_sum(last_ref, 8, 16)
    exp_sum = peer_sum(first_ref, 8, 16)
    row_weight = 1.0 / row_sum
    target_sum = row_weight * row_sum
    cross = jnp.log(exp_sum) * target_sum - row_weight * dot_sum

    counts = count_ref[0:1, :]
    present = jnp.sum(jnp.where(counts > 0.5, 1.0, 0.0), axis=1, keepdims=True)
    count_rows = lanes(counts)
    number = lax.broadcasted_iota(jnp.int32, (LANE, LANE), 0).astype(f32)
    own = [
        jnp.sum(jnp.where(number == lang_ref[k : k + 1, :], count_rows, 0.0), axis=0, keepdims=True)
        for k in range(GROUPS)
    ]
    token_weight = 1.0 / (jnp.concatenate(own, axis=0) * present)
    loss = jnp.sum(jnp.sum(token_weight * cross, axis=1, keepdims=True), axis=0, keepdims=True)
    soft_factor = grad_scale * token_weight * target_sum / exp_sum
    target_factor = grad_scale * token_weight * row_weight
    for k in range(GROUPS):
        a_ref[blk(k), :] = lanes(soft_factor[k : k + 1, :])
        b_ref[blk(k), :] = lanes(target_factor[k : k + 1, :])

    loss_ref[...] = jnp.broadcast_to(loss, (8, LANE))

    def send(chunk):
        cols = pl.ds(chunk * CHUNK, CHUNK)
        return pltpu.make_async_copy(out_ref.at[:, cols], out_hbm.at[:, cols], sems.at[chunk])

    for chunk in range(COLS // CHUNK):
        cols = pl.ds(chunk * CHUNK, CHUNK)
        for k in range(GROUPS):
            a, b = a_ref[blk(k), :], b_ref[blk(k), :]
            for part in range(PARTS):
                j = chunk * PARTS + part
                soft = a * jnp.exp(logit_ref[blk(k), blk(j)] * student_scale)
                target = b * e_ref[blk(k), blk(j)] * col_ref[j : j + 1, :]
                g_ref[blk(k), blk(j)] = (soft - target).astype(bf16)
        full = jnp.dot(turned_ref[...], g_ref[:, cols], preferred_element_type=f32) * student_scale
        w = w_ref[:, cols].astype(f32)
        inv = inv_ref[:, cols]
        inner = jnp.sum(w * full, axis=0, keepdims=True)
        out_ref[:, cols] = (inv * full - w * (inv * inv * inv * inner)).astype(bf16)
        send(chunk).start()
    u_ref[...] = nt(g_ref[...], unit_ref[...])
    core = lax.axis_index("c")
    for x in range(X):
        for ref, c in ((own_ref, core), (send_ref, 1 - core)):
            ref[x] = u_ref[pl.ds(pl.multiple_of((x * C + c) * TOK, TOK), TOK), :]
    for chunk in range(COLS // CHUNK):
        send(chunk).wait()


def add_core(own_ref, other_ref, mine_ref, one_ref, two_ref, three_ref):
    here = lax.axis_index("x")
    for shift, ref in enumerate((mine_ref, one_ref, two_ref, three_ref)):
        x = lax.rem(here + shift, X)
        ref[...] = (own_ref[x] + other_ref[x]).astype(ref.dtype)


def add_x(mine_ref, one_ref, two_ref, three_ref, loss_ref, next_ref, far_ref, last_ref, out_ref, quad_ref):
    total = mine_ref[...] + one_ref[...].astype(f32) + two_ref[...].astype(f32) + three_ref[...].astype(f32)
    out_ref[...] = total.astype(bf16)
    quad_ref[...] = (loss_ref[...] + next_ref[...]) + (far_ref[...] + last_ref[...])


def scatter_rows(
    pos_ref, rows_ref, quad_ref, other_ref, own_ref, one_ref, two_ref, three_ref, out_ref, loss_ref, all_ref
):
    loss_ref[...] = (quad_ref[...] + other_ref[...])[0:1, 0:1]
    y = lax.axis_index("y")
    for shift, ref in enumerate((own_ref, one_ref, two_ref, three_ref)):
        all_ref[lax.rem(y - shift + Y, Y)] = ref[...].astype(f32)
    grad_unit = all_ref[0]
    for other in range(1, Y):
        grad_unit = grad_unit + all_ref[other]
    grad_unit = grad_unit * student_scale
    rows = rows_ref[...]
    row_inv = unit_inverse(rows)
    along = jnp.sum(rows * grad_unit, axis=1, keepdims=True)
    grad_rows = row_inv * grad_unit - rows * (row_inv * row_inv * row_inv) * along
    where = lax.broadcasted_iota(jnp.int32, (FEAT, TOK), 0) == pos_ref[...]
    picker = jnp.where(where, 1.0, 0.0).astype(bf16)
    high, _ = split(grad_rows)
    mid, low = split(grad_rows - high.astype(f32))
    out_ref[...] = (
        jnp.dot(picker, high, preferred_element_type=f32)
        + jnp.dot(picker, mid, preferred_element_type=f32)
        + jnp.dot(picker, low, preferred_element_type=f32)
    )


def add_groups(recv_ref, own_ref, other_ref):
    first = lax.axis_index("c") == 0
    for x in range(X):
        for chunk in range(COLS // CHUNK):
            cols = pl.ds(chunk * CHUNK, CHUNK)
            total = recv_ref[x, :, cols].astype(f32)
            for z in range(1, Z):
                total = total + recv_ref[z * X + x, :, cols].astype(f32)
            there = pl.ds(x * COLS + chunk * CHUNK, CHUNK)
            own_ref[:, there] = jnp.where(first, total[0:4], total[4:8])
            other_ref[:, there] = jnp.where(first, total[4:8], total[0:4])


def join(own_ref, other_ref, out_ref):
    core = lax.axis_index("c")
    for x in range(X):
        for ref, c in ((own_ref, core), (other_ref, 1 - core)):
            there = pl.ds(pl.multiple_of((x * C + c) * COLS, COLS), COLS)
            out_ref[:, there] = ref[:, x * COLS : (x + 1) * COLS]


def exchange(message, axes):
    return lax.all_to_all(message, axes, 0, 0)


def other_core(values):
    return lax.ppermute(values, "c", [(0, 1), (1, 0)])


def shifted(values, axis, size, shift):
    return lax.ppermute(values, axis, [(i, (i + shift) % size) for i in range(size)])


def swapped(values, step):
    return lax.ppermute(values, "z", [(i, i ^ step) for i in range(Z)])


def local(teacher_seq, student_seq, prototypes, positions, languages):
    shape = jax.ShapeDtypeStruct
    kept = pltpu.VMEM
    sems = pltpu.SemaphoreType.DMA
    z_axis, row_axes = ("z",), ("x", "c", "y")
    pos = positions[None, :]

    units, rows = call(
        pick_rows,
        (shape((X, TOK + 16, 2 * FEAT), bf16), shape((TOK, FEAT), f32)),
        [
            pltpu.VMEM((1, TOK), jnp.int32),
            pltpu.VMEM((1, TOK), jnp.int32),
            pltpu.VMEM((FEAT, FEAT), bf16),
            pltpu.VMEM((FEAT, FEAT), bf16),
            sems((4,)),
        ],
        anywhere=(0, 1, 2, 3),
    )(pos, languages[None, :], teacher_seq, student_seq)
    w, unit, inv = call(
        weights,
        (shape((FEAT, COLS), bf16), shape((FEAT, COLS), bf16), shape((1, COLS), f32)),
        [sems((1,))],
        anywhere=(0,),
    )(prototypes)
    totals = pltpu.VMEM((ROWS, LANE), f32)
    products = pltpu.VMEM((ROWS, CHUNK), f32)
    units = exchange(units, ("x",))
    e, logits, turned, lang, count, message = call(
        start,
        (
            kept((ROWS, COLS), f32),
            kept((ROWS, COLS), f32),
            shape((FEAT, ROWS), bf16),
            shape((8, LANE), f32),
            shape((8, LANE), f32),
            shape((PEERS, 16, LANE), f32),
        ),
        [pltpu.VMEM((ROWS, FEAT), bf16), pltpu.VMEM((ROWS, FEAT), bf16), totals, totals, products],
    )(units, other_core(units), unit)

    for sweep in range(ITERS):
        received = exchange(message, row_axes)
        if sweep == 0:
            first = received
        out = shape((Z, 24 if sweep == 0 else 16, LANE), f32)
        message = call(column_pass, out, [pltpu.VMEM((COLS // LANE, 8, LANE), f32)])(received, e, count)
        columns = exchange(message, z_axis)
        if sweep < ITERS - 1:
            small = shape((8, LANE), f32)
            message, *summed = call(row_pass, (shape((PEERS, 8, LANE), f32),) + (small,) * (sweep == 0))(columns, e)
            counts = summed[0] if sweep == 0 else counts
        else:
            message, col = call(row_last, (shape((PEERS, 16, LANE), f32), shape((16, LANE), f32)))(columns, e, logits)
    last = exchange(message, row_axes)
    grad, own, send, loss = call(
        gradients,
        (pltpu.HBM((FEAT, COLS), bf16), shape((X, TOK, FEAT), f32), shape((X, TOK, FEAT), f32), shape((8, LANE), f32)),
        [
            totals,
            totals,
            pltpu.VMEM((ROWS, COLS), bf16),
            pltpu.VMEM((FEAT, COLS), bf16),
            pltpu.VMEM((ROWS, FEAT), f32),
            sems((COLS // CHUNK,)),
        ],
        out_anywhere=(0,),
    )(last, first, lang, counts, e, logits, col, turned, unit, w, inv)
    block = shape((TOK, FEAT), f32)
    short = shape((TOK, FEAT), bf16)
    mine, *parts = call(add_core, (block, short, short, short))(own, other_core(send))
    pieces = [shifted(part, "x", X, s) for s, part in enumerate(parts, 1)]
    losses = [swapped(loss, step) for step in (1, 2, 3)]
    mine, quad = call(add_x, (short, shape((8, LANE), f32)))(mine, *pieces, loss, *losses)
    others = [shifted(mine, "y", Y, s) for s in range(1, Y)]
    grad = exchange(grad.reshape(Z * X, 8, COLS), ("z", "x"))
    grad_student, loss = call(
        scatter_rows,
        (shape((FEAT, FEAT), f32), shape((1, 1), f32)),
        [pltpu.VMEM((Y, TOK, FEAT), f32)],
    )(pos, rows, quad, swapped(quad, 4), mine, *others)
    grad, grad_student = lax.optimization_barrier((grad, grad_student))
    half = shape((4, X * COLS), f32)
    mine, theirs = call(add_groups, (half, half))(grad)
    grad_prototypes = call(join, shape((4, GROUPS * COLS), f32))(mine, other_core(theirs))
    return (loss[0, 0], grad_student, grad_prototypes)


def solution(mesh):
    fine = Mesh(mesh.devices.reshape(Z, X, C, Y), ("z", "x", "c", "y"))
    tok = ("z", "x", "c")
    in_specs = (P(tok, None), P(tok, None), P(None, "y"), P(tok), P(tok))
    out_specs = (P(), P(tok, None), P(tok, "y"))
    return jax.shard_map(local, mesh=fine, in_specs=in_specs, out_specs=out_specs, check_vma=False)
```

```python
import jax
import jax.numpy as jnp
from jax import lax
from jax.experimental import pallas as pl
from jax.experimental.pallas import tpu as pltpu
from jax.sharding import Mesh, PartitionSpec as P

LANGS = 100
ITERS = 3

epsilon = 1e-06
teacher_scale = 20.0
student_scale = 10.0
grad_scale = 8388608.0

Z, X, C, Y = 8, 4, 2, 4
TOK = 128
GROUPS = X * C
ROWS = GROUPS * TOK
COLS = 2048
FEAT = 256
LANE = 128
CHUNK = 512
PARTS = CHUNK // LANE
PEERS = X * C * Y
LOSS_LANES = 128
f32 = jnp.float32
bf16 = jnp.bfloat16


def call(kernel, out_shape, scratch=(), anywhere=(), out_anywhere=(), mib=24):
    def run(*args):
        space = lambda far: pl.BlockSpec(memory_space=pltpu.HBM if far else pltpu.VMEM)
        args = [pltpu.with_memory_space_constraint(a, pltpu.HBM) if i in anywhere else a for i, a in enumerate(args)]
        multiple = isinstance(out_shape, (tuple, list))
        outs = [space(i in out_anywhere) for i in range(len(out_shape) if multiple else 1)]
        return pl.pallas_call(
            kernel,
            out_shape=out_shape,
            in_specs=[space(i in anywhere) for i in range(len(args))],
            out_specs=outs if multiple else outs[0],
            scratch_shapes=list(scratch),
            compiler_params=pltpu.CompilerParams(vmem_limit_bytes=mib << 20),
            name=kernel.__name__,
        )(*args)

    return run


def lanes(row):
    return jnp.broadcast_to(row, (LANE, LANE)).T


def row_totals(block):
    return jnp.sum(block.T, axis=0, keepdims=True)


def blk(index):
    return pl.ds(index * LANE, LANE)


def split(values):
    high = values.astype(bf16)
    return high, (values - high.astype(f32)).astype(bf16)


def nt(left, right):
    return lax.dot_general(left, right, (((1,), (1,)), ((), ())), preferred_element_type=f32)


def tn(left, right):
    return lax.dot_general(left, right, (((0,), (0,)), ((), ())), preferred_element_type=f32)


def unit_inverse(values):
    return lax.rsqrt(jnp.sum(values * values, axis=1, keepdims=True) + epsilon)


def fetch(sources, targets, sems):
    copies = [pltpu.make_async_copy(a, b, sems.at[n]) for n, (a, b) in enumerate(zip(sources, targets))]
    for copy in copies:
        copy.start()
    for copy in copies:
        copy.wait()


def pick_rows(pos_hbm, lang_hbm, teacher_hbm, student_hbm, out_ref, rows_ref, pos_ref, lang_ref, teacher_ref, student_ref, sems):
    fetch((pos_hbm, lang_hbm, teacher_hbm, student_hbm), (pos_ref, lang_ref, teacher_ref, student_ref), sems)
    where = lax.broadcasted_iota(jnp.int32, (FEAT, TOK), 0) == pos_ref[...]
    picker = jnp.where(where, 1.0, 0.0).astype(bf16)
    teacher = tn(picker, teacher_ref[...])
    student = tn(picker, student_ref[...])
    teacher_unit = (teacher * unit_inverse(teacher)).astype(bf16)
    student_unit = (student * unit_inverse(student)).astype(bf16)
    language = jnp.broadcast_to(lang_ref[...].astype(f32), (16, TOK)).astype(bf16)
    rows_ref[...] = student
    for peer in range(X):
        out_ref[peer, 0:TOK, 0:FEAT] = teacher_unit
        out_ref[peer, 0:TOK, FEAT : 2 * FEAT] = student_unit
        for part in range(4):
            out_ref[peer, TOK : TOK + 16, part * LANE : (part + 1) * LANE] = language


def weights(proto_hbm, w_ref, unit_ref, inv_ref, sems):
    group = lax.axis_index("x") * C + lax.axis_index("c")
    here = pl.ds(pl.multiple_of(group * COLS, COLS), COLS)
    fetch((proto_hbm.at[:, here],), (w_ref,), sems)
    for chunk in range(COLS // CHUNK):
        cols = pl.ds(chunk * CHUNK, CHUNK)
        w = w_ref[:, cols].astype(f32)
        inv = lax.rsqrt(jnp.sum(w * w, axis=0, keepdims=True) + epsilon)
        inv_ref[:, cols] = inv
        unit_ref[:, cols] = (w * inv).astype(bf16)


def lane_sum(block):
    total = block[:, 0:LANE]
    for part in range(1, PARTS):
        total = total + block[:, part * LANE : (part + 1) * LANE]
    return total


def all_row_totals(acc_ref):
    return jnp.concatenate([row_totals(acc_ref[blk(k), :]) for k in range(GROUPS)], axis=0)


def start(
    own_ref, other_ref, unit_ref, e_ref, logit_ref, turned_ref, lang_ref, count_ref, msg_ref, rest_ref,
    teacher_ref, student_ref, acc_ref, exp_ref, d_ref,
):
    core = lax.axis_index("c")
    for x in range(X):
        for ref, c in ((own_ref, core), (other_ref, 1 - core)):
            here = pl.ds(pl.multiple_of((x * C + c) * TOK, TOK), TOK)
            teacher_ref[here, :] = ref[x, 0:TOK, 0:FEAT]
            student_ref[here, :] = ref[x, 0:TOK, FEAT : 2 * FEAT]
            lang_ref[pl.ds(x * C + c, 1), :] = ref[x, TOK : TOK + 16, 0:LANE].astype(f32)[0:1, :]
    for k in range(GROUPS):
        turned_ref[:, blk(k)] = student_ref[blk(k), :].astype(f32).T.astype(bf16)
    hits = jnp.zeros((LANE, LANE), f32)
    number = lax.broadcasted_iota(jnp.int32, (LANE, LANE), 0).astype(f32)
    for k in range(GROUPS):
        hits = hits + jnp.where(number == lang_ref[k : k + 1, :], 1.0, 0.0)
    count_ref[...] = jnp.broadcast_to(row_totals(hits), (8, LANE))
    acc_ref[...] = jnp.zeros((ROWS, LANE), f32)
    exp_ref[...] = jnp.zeros((ROWS, LANE), f32)

    def step(chunk):
        cols = pl.ds(chunk * CHUNK, CHUNK)
        unit = unit_ref[:, cols]
        d_ref[...] = jnp.dot(teacher_ref[...], unit, preferred_element_type=f32)
        logit_ref[:, cols] = jnp.dot(student_ref[...], unit, preferred_element_type=f32)
        for k in range(GROUPS):
            e = jnp.exp(d_ref[blk(k), :] * teacher_scale)
            e_ref[blk(k), cols] = e
            acc_ref[blk(k), :] += lane_sum(e)
            exp_ref[blk(k), :] += lane_sum(jnp.exp(logit_ref[blk(k), cols] * student_scale))

    for chunk in range(COLS // CHUNK):
        step(chunk)
    high, rest = split(all_row_totals(exp_ref))
    rest_ref[...] = rest.astype(f32)
    send_pair(msg_ref, all_row_totals(acc_ref), high.astype(f32))


def send_rows(msg_ref, *parts):
    for peer in range(PEERS):
        for n, part in enumerate(parts):
            msg_ref[peer, 8 * n : 8 * n + 8, :] = part


def send_pair(msg_ref, first, second):
    both = jnp.concatenate([first, second], axis=0).astype(bf16)
    for peer in range(PEERS):
        msg_ref[peer] = both


def peer_sum(recv_ref, low, high):
    total = recv_ref[0, low:high, :].astype(f32)
    for peer in range(1, recv_ref.shape[0]):
        total = total + recv_ref[peer, low:high, :].astype(f32)
    return total


def column_pass(recv_ref, e_ref, count_ref, msg_ref, acc_ref):
    rows = 16 if recv_ref.dtype == bf16 else 8
    row_weight = 1.0 / peer_sum(recv_ref, 0, rows)[0:8]
    for k in range(GROUPS):
        factor = lanes(row_weight[k : k + 1, :])
        for j in range(COLS // LANE):
            part = jnp.sum((e_ref[blk(k), blk(j)] * factor).reshape(LANE // 8, 8, LANE), axis=0)
            acc_ref[j] = part if k == 0 else acc_ref[j] + part
    sums = jnp.concatenate([jnp.sum(acc_ref[j], axis=0, keepdims=True) for j in range(COLS // LANE)], axis=0)
    for peer in range(Z):
        msg_ref[peer, 0:16, :] = sums
        if msg_ref.shape[1] > 16:
            msg_ref[peer, 16:24, :] = count_ref[...]


def weighted_rows(e_ref, col_weight):
    out = []
    for k in range(GROUPS):
        acc = e_ref[blk(k), blk(0)] * col_weight[0:1, :]
        for j in range(1, COLS // LANE):
            acc = acc + e_ref[blk(k), blk(j)] * col_weight[j : j + 1, :]
        out.append(row_totals(acc))
    return jnp.concatenate(out, axis=0)


def row_first(recv_ref, e_ref, rest_ref, msg_ref, count_ref):
    count_ref[...] = peer_sum(recv_ref, 16, 24)
    send_pair(msg_ref, weighted_rows(e_ref, 1.0 / peer_sum(recv_ref, 0, 16)), rest_ref[...])


def row_pass(recv_ref, e_ref, msg_ref):
    send_rows(msg_ref, weighted_rows(e_ref, 1.0 / peer_sum(recv_ref, 0, 16)))


def row_last(recv_ref, e_ref, logit_ref, msg_ref, col_ref):
    col_weight = 1.0 / peer_sum(recv_ref, 0, 16)
    col_ref[...] = col_weight
    sums, dots = [], []
    for k in range(GROUPS):
        total = e_ref[blk(k), blk(0)] * col_weight[0:1, :]
        dot = total * logit_ref[blk(k), blk(0)]
        for j in range(1, COLS // LANE):
            t = e_ref[blk(k), blk(j)] * col_weight[j : j + 1, :]
            total = total + t
            dot = dot + t * logit_ref[blk(k), blk(j)]
        sums.append(row_totals(total))
        dots.append(row_totals(dot) * student_scale)
    send_rows(msg_ref, jnp.concatenate(sums, axis=0), jnp.concatenate(dots, axis=0))


def gradients(
    last_ref, first_ref, second_ref, lang_ref, count_ref, e_ref, logit_ref, col_ref, turned_ref, unit_ref, w_ref, inv_ref,
    out_hbm, own_ref, send_ref, a_ref, b_ref, g_ref, out_ref, u_ref, sems,
):
    row_sum = peer_sum(last_ref, 0, 8)
    dot_sum = peer_sum(last_ref, 8, 16)
    exp_sum = peer_sum(first_ref, 0, 16)[8:16] + peer_sum(second_ref, 0, 16)[8:16]
    row_weight = 1.0 / row_sum
    target_sum = row_weight * row_sum
    cross = jnp.log(exp_sum) * target_sum - row_weight * dot_sum

    counts = count_ref[0:1, :]
    present = jnp.sum(jnp.where(counts > 0.5, 1.0, 0.0), axis=1, keepdims=True)
    count_rows = lanes(counts)
    number = lax.broadcasted_iota(jnp.int32, (LANE, LANE), 0).astype(f32)
    own = [
        jnp.sum(jnp.where(number == lang_ref[k : k + 1, :], count_rows, 0.0), axis=0, keepdims=True)
        for k in range(GROUPS)
    ]
    token_weight = 1.0 / (jnp.concatenate(own, axis=0) * present)
    loss = jnp.sum(jnp.sum(token_weight * cross, axis=1, keepdims=True), axis=0, keepdims=True)
    soft_factor = grad_scale * token_weight * target_sum / exp_sum
    target_factor = grad_scale * token_weight * row_weight
    for k in range(GROUPS):
        a_ref[blk(k), :] = lanes(soft_factor[k : k + 1, :])
        b_ref[blk(k), :] = lanes(target_factor[k : k + 1, :])

    def send(chunk, width):
        cols = pl.ds(pl.multiple_of(chunk * CHUNK, CHUNK), width)
        return pltpu.make_async_copy(out_ref.at[:, cols], out_hbm.at[:, cols], sems.at[chunk])

    loss_high, _ = split(loss)
    loss_mid, loss_low = split(loss - loss_high.astype(f32))
    lane = lax.broadcasted_iota(jnp.int32, (FEAT, LANE), 1)
    packed = jnp.where(lane == 0, loss_high.astype(f32), jnp.where(lane == 1, loss_mid.astype(f32), loss_low.astype(f32)))
    out_ref[:, COLS : COLS + LANE] = packed.astype(bf16)
    send(COLS // CHUNK, LOSS_LANES).start()

    for chunk in range(COLS // CHUNK):
        cols = pl.ds(chunk * CHUNK, CHUNK)
        for k in range(GROUPS):
            a, b = a_ref[blk(k), :], b_ref[blk(k), :]
            for part in range(PARTS):
                j = chunk * PARTS + part
                soft = a * jnp.exp(logit_ref[blk(k), blk(j)] * student_scale)
                target = b * e_ref[blk(k), blk(j)] * col_ref[j : j + 1, :]
                g_ref[blk(k), blk(j)] = (soft - target).astype(bf16)
        full = jnp.dot(turned_ref[...], g_ref[:, cols], preferred_element_type=f32) * student_scale
        w = w_ref[:, cols].astype(f32)
        inv = inv_ref[:, cols]
        inner = jnp.sum(w * full, axis=0, keepdims=True)
        out_ref[:, cols] = (inv * full - w * (inv * inv * inv * inner)).astype(bf16)
        send(chunk, CHUNK).start()
    u_ref[...] = nt(g_ref[...], unit_ref[...])
    core = lax.axis_index("c")
    for x in range(X):
        for ref, c in ((own_ref, core), (send_ref, 1 - core)):
            ref[x] = u_ref[pl.ds(pl.multiple_of((x * C + c) * TOK, TOK), TOK), :]
    for chunk in range(COLS // CHUNK):
        send(chunk, CHUNK).wait()
    send(COLS // CHUNK, LOSS_LANES).wait()


def add_core(own_ref, other_ref, mine_ref, one_ref, two_ref, three_ref):
    here = lax.axis_index("x")
    for shift, ref in enumerate((mine_ref, one_ref, two_ref, three_ref)):
        x = lax.rem(here + shift, X)
        ref[...] = (own_ref[x] + other_ref[x]).astype(ref.dtype)


def add_x(mine_ref, one_ref, two_ref, three_ref, out_ref):
    total = mine_ref[...] + one_ref[...].astype(f32) + two_ref[...].astype(f32) + three_ref[...].astype(f32)
    out_ref[...] = total.astype(bf16)


def scatter_rows(pos_ref, rows_ref, own_ref, one_ref, two_ref, three_ref, out_ref, all_ref):
    y = lax.axis_index("y")
    for shift, ref in enumerate((own_ref, one_ref, two_ref, three_ref)):
        all_ref[lax.rem(y - shift + Y, Y)] = ref[...].astype(f32)
    grad_unit = all_ref[0]
    for other in range(1, Y):
        grad_unit = grad_unit + all_ref[other]
    grad_unit = grad_unit * student_scale
    rows = rows_ref[...]
    row_inv = unit_inverse(rows)
    along = jnp.sum(rows * grad_unit, axis=1, keepdims=True)
    grad_rows = row_inv * grad_unit - rows * (row_inv * row_inv * row_inv) * along
    where = lax.broadcasted_iota(jnp.int32, (FEAT, TOK), 0) == pos_ref[...]
    picker = jnp.where(where, 1.0, 0.0).astype(bf16)
    high, _ = split(grad_rows)
    mid, low = split(grad_rows - high.astype(f32))
    out_ref[...] = (
        jnp.dot(picker, high, preferred_element_type=f32)
        + jnp.dot(picker, mid, preferred_element_type=f32)
        + jnp.dot(picker, low, preferred_element_type=f32)
    )


def add_groups(recv_ref, own_ref, other_ref, loss_ref):
    first = lax.axis_index("c") == 0
    for x in range(X):
        for chunk in range(COLS // CHUNK):
            cols = pl.ds(chunk * CHUNK, CHUNK)
            total = recv_ref[x, :, cols].astype(f32)
            for z in range(1, Z):
                total = total + recv_ref[z * X + x, :, cols].astype(f32)
            there = pl.ds(x * COLS + chunk * CHUNK, CHUNK)
            own_ref[:, there] = jnp.where(first, total[0:4], total[4:8])
            other_ref[:, there] = jnp.where(first, total[4:8], total[0:4])
    loss = recv_ref[0, :, COLS : COLS + LANE].astype(f32)
    for z in range(1, Z):
        loss = loss + recv_ref[z * X, :, COLS : COLS + LANE].astype(f32)
    lane = lax.broadcasted_iota(jnp.int32, loss.shape, 1)
    loss_ref[...] = jnp.sum(jnp.where(lane < 3, loss, 0.0)[0:1, :], axis=1, keepdims=True)


def join(own_ref, other_ref, out_ref):
    core = lax.axis_index("c")
    for x in range(X):
        for ref, c in ((own_ref, core), (other_ref, 1 - core)):
            there = pl.ds(pl.multiple_of((x * C + c) * COLS, COLS), COLS)
            out_ref[:, there] = ref[:, x * COLS : (x + 1) * COLS]


def exchange(message, axes):
    return lax.all_to_all(message, axes, 0, 0)


def other_core(values):
    return lax.ppermute(values, "c", [(0, 1), (1, 0)])


def shifted(values, axis, size, shift):
    return lax.ppermute(values, axis, [(i, (i + shift) % size) for i in range(size)])


def local(teacher_seq, student_seq, prototypes, positions, languages):
    shape = jax.ShapeDtypeStruct
    kept = pltpu.VMEM
    sems = pltpu.SemaphoreType.DMA
    z_axis, row_axes = ("z",), ("x", "c", "y")
    pos = positions[None, :]

    units, rows = call(
        pick_rows,
        (shape((X, TOK + 16, 2 * FEAT), bf16), shape((TOK, FEAT), f32)),
        [
            pltpu.VMEM((1, TOK), jnp.int32),
            pltpu.VMEM((1, TOK), jnp.int32),
            pltpu.VMEM((FEAT, FEAT), bf16),
            pltpu.VMEM((FEAT, FEAT), bf16),
            sems((4,)),
        ],
        anywhere=(0, 1, 2, 3),
    )(pos, languages[None, :], teacher_seq, student_seq)
    w, unit, inv = call(
        weights,
        (shape((FEAT, COLS), bf16), shape((FEAT, COLS), bf16), shape((1, COLS), f32)),
        [sems((1,))],
        anywhere=(0,),
    )(prototypes)
    totals = pltpu.VMEM((ROWS, LANE), f32)
    products = pltpu.VMEM((ROWS, CHUNK), f32)
    small = shape((8, LANE), f32)
    units = exchange(units, ("x",))
    e, logits, turned, lang, count, message, rest = call(
        start,
        (
            kept((ROWS, COLS), f32),
            kept((ROWS, COLS), f32),
            shape((FEAT, ROWS), bf16),
            shape((8, LANE), f32),
            shape((8, LANE), f32),
            shape((PEERS, 16, LANE), bf16),
            small,
        ),
        [pltpu.VMEM((ROWS, FEAT), bf16), pltpu.VMEM((ROWS, FEAT), bf16), totals, totals, products],
    )(units, other_core(units), unit)

    arrived = []
    for sweep in range(ITERS):
        arrived.append(exchange(message, row_axes))
        out = shape((Z, 24 if sweep == 0 else 16, LANE), f32)
        message = call(column_pass, out, [pltpu.VMEM((COLS // LANE, 8, LANE), f32)])(arrived[-1], e, count)
        columns = exchange(message, z_axis)
        if sweep == 0:
            message, counts = call(row_first, (shape((PEERS, 16, LANE), bf16), small))(columns, e, rest)
        elif sweep < ITERS - 1:
            message = call(row_pass, shape((PEERS, 8, LANE), f32))(columns, e)
        else:
            message, col = call(row_last, (shape((PEERS, 16, LANE), f32), shape((16, LANE), f32)))(columns, e, logits)
    last = exchange(message, row_axes)
    grad, own, send = call(
        gradients,
        (pltpu.HBM((FEAT, COLS + LOSS_LANES), bf16), shape((X, TOK, FEAT), f32), shape((X, TOK, FEAT), f32)),
        [
            totals,
            totals,
            pltpu.VMEM((ROWS, COLS), bf16),
            pltpu.VMEM((FEAT, COLS + LOSS_LANES), bf16),
            pltpu.VMEM((ROWS, FEAT), f32),
            sems((COLS // CHUNK + 1,)),
        ],
        out_anywhere=(0,),
    )(last, arrived[0], arrived[1], lang, counts, e, logits, col, turned, unit, w, inv)
    block = shape((TOK, FEAT), f32)
    short = shape((TOK, FEAT), bf16)
    mine, *parts = call(add_core, (block, short, short, short))(own, other_core(send))
    mine = call(add_x, short)(mine, *(shifted(part, "x", X, s) for s, part in enumerate(parts, 1)))
    others = [shifted(mine, "y", Y, s) for s in range(1, Y)]
    grad = exchange(grad.reshape(Z * X, 8, COLS + LOSS_LANES), ("z", "x"))
    grad_student = call(
        scatter_rows,
        shape((FEAT, FEAT), f32),
        [pltpu.VMEM((Y, TOK, FEAT), f32)],
    )(pos, rows, mine, *others)
    grad, grad_student = lax.optimization_barrier((grad, grad_student))
    half = shape((4, X * COLS), f32)
    mine, theirs, loss = call(add_groups, (half, half, shape((1, 1), f32)))(grad)
    grad_prototypes = call(join, shape((4, GROUPS * COLS), f32))(mine, other_core(theirs))
    return (loss[0, 0], grad_student, grad_prototypes)


def solution(mesh):
    fine = Mesh(mesh.devices.reshape(Z, X, C, Y), ("z", "x", "c", "y"))
    tok = ("z", "x", "c")
    in_specs = (P(tok, None), P(tok, None), P(None, "y"), P(tok), P(tok))
    out_specs = (P(), P(tok, None), P(tok, "y"))
    return jax.shard_map(local, mesh=fine, in_specs=in_specs, out_specs=out_specs, check_vma=False)
```

```python
import jax
import jax.numpy as jnp
from jax import lax
from jax.experimental import pallas as pl
from jax.experimental.pallas import tpu as pltpu
from jax.sharding import Mesh, PartitionSpec as P

LANGS = 100
ITERS = 3

epsilon = 1e-06
teacher_scale = 20.0
student_scale = 10.0
grad_scale = 8388608.0

Z, X, C, Y = 8, 4, 2, 4
TOK = 128
GROUPS = X * C
ROWS = GROUPS * TOK
COLS = 2048
FEAT = 256
LANE = 128
CHUNK = 512
PARTS = CHUNK // LANE
PEERS = X * C * Y
LOSS_LANES = 128
f32 = jnp.float32
bf16 = jnp.bfloat16


def call(kernel, out_shape, scratch=(), anywhere=(), out_anywhere=(), mib=24):
    def run(*args):
        space = lambda far: pl.BlockSpec(memory_space=pltpu.HBM if far else pltpu.VMEM)
        args = [pltpu.with_memory_space_constraint(a, pltpu.HBM) if i in anywhere else a for i, a in enumerate(args)]
        multiple = isinstance(out_shape, (tuple, list))
        outs = [space(i in out_anywhere) for i in range(len(out_shape) if multiple else 1)]
        return pl.pallas_call(
            kernel,
            out_shape=out_shape,
            in_specs=[space(i in anywhere) for i in range(len(args))],
            out_specs=outs if multiple else outs[0],
            scratch_shapes=list(scratch),
            compiler_params=pltpu.CompilerParams(vmem_limit_bytes=mib << 20),
            name=kernel.__name__,
        )(*args)

    return run


def lanes(row):
    return jnp.broadcast_to(row, (LANE, LANE)).T


def row_totals(block):
    return jnp.sum(block.T, axis=0, keepdims=True)


def blk(index):
    return pl.ds(index * LANE, LANE)


def split(values):
    high = values.astype(bf16)
    return high, (values - high.astype(f32)).astype(bf16)


def nt(left, right):
    return lax.dot_general(left, right, (((1,), (1,)), ((), ())), preferred_element_type=f32)


def tn(left, right):
    return lax.dot_general(left, right, (((0,), (0,)), ((), ())), preferred_element_type=f32)


def unit_inverse(values):
    return lax.rsqrt(jnp.sum(values * values, axis=1, keepdims=True) + epsilon)


def fetch(sources, targets, sems):
    copies = [pltpu.make_async_copy(a, b, sems.at[n]) for n, (a, b) in enumerate(zip(sources, targets))]
    for copy in copies:
        copy.start()
    for copy in copies:
        copy.wait()


def pick_rows(pos_hbm, lang_hbm, teacher_hbm, student_hbm, out_ref, rows_ref, pos_ref, lang_ref, teacher_ref, student_ref, sems):
    fetch((pos_hbm, lang_hbm, teacher_hbm, student_hbm), (pos_ref, lang_ref, teacher_ref, student_ref), sems)
    where = lax.broadcasted_iota(jnp.int32, (FEAT, TOK), 0) == pos_ref[...]
    picker = jnp.where(where, 1.0, 0.0).astype(bf16)
    teacher = tn(picker, teacher_ref[...])
    student = tn(picker, student_ref[...])
    teacher_unit = (teacher * unit_inverse(teacher)).astype(bf16)
    student_unit = (student * unit_inverse(student)).astype(bf16)
    language = jnp.broadcast_to(lang_ref[...].astype(f32), (16, TOK)).astype(bf16)
    rows_ref[...] = student
    for peer in range(X):
        out_ref[peer, 0:TOK, 0:FEAT] = teacher_unit
        out_ref[peer, 0:TOK, FEAT : 2 * FEAT] = student_unit
        for part in range(4):
            out_ref[peer, TOK : TOK + 16, part * LANE : (part + 1) * LANE] = language


def weights(proto_hbm, w_ref, unit_ref, inv_ref, sems):
    group = lax.axis_index("x") * C + lax.axis_index("c")
    here = pl.ds(pl.multiple_of(group * COLS, COLS), COLS)
    fetch((proto_hbm.at[:, here],), (w_ref,), sems)
    for chunk in range(COLS // CHUNK):
        cols = pl.ds(chunk * CHUNK, CHUNK)
        w = w_ref[:, cols].astype(f32)
        inv = lax.rsqrt(jnp.sum(w * w, axis=0, keepdims=True) + epsilon)
        inv_ref[:, cols] = inv
        unit_ref[:, cols] = (w * inv).astype(bf16)


def lane_sum(block):
    total = block[:, 0:LANE]
    for part in range(1, PARTS):
        total = total + block[:, part * LANE : (part + 1) * LANE]
    return total


def all_row_totals(acc_ref):
    return jnp.concatenate([row_totals(acc_ref[blk(k), :]) for k in range(GROUPS)], axis=0)


def start(
    own_ref, other_ref, unit_ref, e_ref, logit_ref, turned_ref, lang_ref, count_ref, msg_ref, rest_ref,
    teacher_ref, student_ref, acc_ref, exp_ref, d_ref,
):
    core = lax.axis_index("c")
    for x in range(X):
        for ref, c in ((own_ref, core), (other_ref, 1 - core)):
            here = pl.ds(pl.multiple_of((x * C + c) * TOK, TOK), TOK)
            teacher_ref[here, :] = ref[x, 0:TOK, 0:FEAT]
            student_ref[here, :] = ref[x, 0:TOK, FEAT : 2 * FEAT]
            lang_ref[pl.ds(x * C + c, 1), :] = ref[x, TOK : TOK + 16, 0:LANE].astype(f32)[0:1, :]
    for k in range(GROUPS):
        turned_ref[:, blk(k)] = student_ref[blk(k), :].astype(f32).T.astype(bf16)
    hits = jnp.zeros((LANE, LANE), f32)
    number = lax.broadcasted_iota(jnp.int32, (LANE, LANE), 0).astype(f32)
    for k in range(GROUPS):
        hits = hits + jnp.where(number == lang_ref[k : k + 1, :], 1.0, 0.0)
    count_ref[...] = jnp.broadcast_to(row_totals(hits), (8, LANE))
    acc_ref[...] = jnp.zeros((ROWS, LANE), f32)
    exp_ref[...] = jnp.zeros((ROWS, LANE), f32)

    def step(chunk):
        cols = pl.ds(chunk * CHUNK, CHUNK)
        unit = unit_ref[:, cols]
        d_ref[...] = jnp.dot(teacher_ref[...], unit, preferred_element_type=f32)
        logit_ref[:, cols] = jnp.dot(student_ref[...], unit, preferred_element_type=f32)
        for k in range(GROUPS):
            e = jnp.exp(d_ref[blk(k), :] * teacher_scale)
            e_ref[blk(k), cols] = e
            acc_ref[blk(k), :] += lane_sum(e)
            exp_ref[blk(k), :] += lane_sum(jnp.exp(logit_ref[blk(k), cols] * student_scale))

    for chunk in range(COLS // CHUNK):
        step(chunk)
    high, rest = split(all_row_totals(exp_ref))
    rest_ref[...] = rest.astype(f32)
    send_pair(msg_ref, all_row_totals(acc_ref), high.astype(f32))


def send_rows(msg_ref, *parts):
    for peer in range(PEERS):
        for n, part in enumerate(parts):
            msg_ref[peer, 8 * n : 8 * n + 8, :] = part


def two_parts(values):
    high, low = split(values)
    return jnp.concatenate([high.astype(f32), low.astype(f32)], axis=0).astype(bf16)


def send_pair(msg_ref, first, second):
    both = jnp.concatenate([first, second], axis=0).astype(bf16)
    for peer in range(PEERS):
        msg_ref[peer] = both


def peer_sum(recv_ref, low, high):
    total = recv_ref[0, low:high, :].astype(f32)
    for peer in range(1, recv_ref.shape[0]):
        total = total + recv_ref[peer, low:high, :].astype(f32)
    return total


def column_pass(recv_ref, e_ref, count_ref, msg_ref, acc_ref):
    rows = 16 if recv_ref.dtype == bf16 else 8
    row_weight = 1.0 / peer_sum(recv_ref, 0, rows)[0:8]
    for k in range(GROUPS):
        factor = lanes(row_weight[k : k + 1, :])
        for j in range(COLS // LANE):
            part = jnp.sum((e_ref[blk(k), blk(j)] * factor).reshape(LANE // 8, 8, LANE), axis=0)
            acc_ref[j] = part if k == 0 else acc_ref[j] + part
    sums = jnp.concatenate([jnp.sum(acc_ref[j], axis=0, keepdims=True) for j in range(COLS // LANE)], axis=0)
    counts = two_parts(count_ref[...])
    for peer in range(Z):
        msg_ref[peer, 0:16, :] = sums.astype(msg_ref.dtype)
        if msg_ref.shape[1] > 16:
            msg_ref[peer, 16:32, :] = counts


def weighted_rows(e_ref, col_weight):
    out = []
    for k in range(GROUPS):
        acc = e_ref[blk(k), blk(0)] * col_weight[0:1, :]
        for j in range(1, COLS // LANE):
            acc = acc + e_ref[blk(k), blk(j)] * col_weight[j : j + 1, :]
        out.append(row_totals(acc))
    return jnp.concatenate(out, axis=0)


def row_first(recv_ref, e_ref, rest_ref, msg_ref, count_ref):
    counts = peer_sum(recv_ref, 16, 32)
    count_ref[...] = counts[0:8] + counts[8:16]
    send_pair(msg_ref, weighted_rows(e_ref, 1.0 / peer_sum(recv_ref, 0, 16)), rest_ref[...])


def row_pass(recv_ref, e_ref, msg_ref):
    send_rows(msg_ref, weighted_rows(e_ref, 1.0 / peer_sum(recv_ref, 0, 16)))


def row_last(recv_ref, e_ref, logit_ref, msg_ref, col_ref):
    col_weight = 1.0 / peer_sum(recv_ref, 0, 16)
    col_ref[...] = col_weight
    sums, dots = [], []
    for k in range(GROUPS):
        total = e_ref[blk(k), blk(0)] * col_weight[0:1, :]
        dot = total * logit_ref[blk(k), blk(0)]
        for j in range(1, COLS // LANE):
            t = e_ref[blk(k), blk(j)] * col_weight[j : j + 1, :]
            total = total + t
            dot = dot + t * logit_ref[blk(k), blk(j)]
        sums.append(row_totals(total))
        dots.append(row_totals(dot) * student_scale)
    send_rows(msg_ref, jnp.concatenate(sums, axis=0), jnp.concatenate(dots, axis=0))


def gradients(
    last_ref, first_ref, second_ref, lang_ref, count_ref, e_ref, logit_ref, col_ref, turned_ref, unit_ref, w_ref, inv_ref,
    out_hbm, own_ref, send_ref, a_ref, b_ref, g_ref, out_ref, u_ref, sems,
):
    row_sum = peer_sum(last_ref, 0, 8)
    dot_sum = peer_sum(last_ref, 8, 16)
    exp_sum = peer_sum(first_ref, 0, 16)[8:16] + peer_sum(second_ref, 0, 16)[8:16]
    row_weight = 1.0 / row_sum
    target_sum = row_weight * row_sum
    cross = jnp.log(exp_sum) * target_sum - row_weight * dot_sum

    counts = count_ref[0:1, :]
    present = jnp.sum(jnp.where(counts > 0.5, 1.0, 0.0), axis=1, keepdims=True)
    count_rows = lanes(counts)
    number = lax.broadcasted_iota(jnp.int32, (LANE, LANE), 0).astype(f32)
    own = [
        jnp.sum(jnp.where(number == lang_ref[k : k + 1, :], count_rows, 0.0), axis=0, keepdims=True)
        for k in range(GROUPS)
    ]
    token_weight = 1.0 / (jnp.concatenate(own, axis=0) * present)
    loss = jnp.sum(jnp.sum(token_weight * cross, axis=1, keepdims=True), axis=0, keepdims=True)
    soft_factor = grad_scale * token_weight * target_sum / exp_sum
    target_factor = grad_scale * token_weight * row_weight
    for k in range(GROUPS):
        a_ref[blk(k), :] = lanes(soft_factor[k : k + 1, :])
        b_ref[blk(k), :] = lanes(target_factor[k : k + 1, :])

    def send(chunk, width):
        cols = pl.ds(pl.multiple_of(chunk * CHUNK, CHUNK), width)
        return pltpu.make_async_copy(out_ref.at[:, cols], out_hbm.at[:, cols], sems.at[chunk])

    loss_high, _ = split(loss)
    loss_mid, loss_low = split(loss - loss_high.astype(f32))
    lane = lax.broadcasted_iota(jnp.int32, (FEAT, LANE), 1)
    packed = jnp.where(lane == 0, loss_high.astype(f32), jnp.where(lane == 1, loss_mid.astype(f32), loss_low.astype(f32)))
    out_ref[:, COLS : COLS + LANE] = packed.astype(bf16)
    send(COLS // CHUNK, LOSS_LANES).start()

    for chunk in range(COLS // CHUNK):
        cols = pl.ds(chunk * CHUNK, CHUNK)
        for k in range(GROUPS):
            a, b = a_ref[blk(k), :], b_ref[blk(k), :]
            for part in range(PARTS):
                j = chunk * PARTS + part
                soft = a * jnp.exp(logit_ref[blk(k), blk(j)] * student_scale)
                target = b * e_ref[blk(k), blk(j)] * col_ref[j : j + 1, :]
                g_ref[blk(k), blk(j)] = (soft - target).astype(bf16)
        full = jnp.dot(turned_ref[...], g_ref[:, cols], preferred_element_type=f32) * student_scale
        w = w_ref[:, cols].astype(f32)
        inv = inv_ref[:, cols]
        inner = jnp.sum(w * full, axis=0, keepdims=True)
        out_ref[:, cols] = (inv * full - w * (inv * inv * inv * inner)).astype(bf16)
        send(chunk, CHUNK).start()
    u_ref[...] = nt(g_ref[...], unit_ref[...])
    core = lax.axis_index("c")
    for x in range(X):
        for ref, c in ((own_ref, core), (send_ref, 1 - core)):
            ref[x] = u_ref[pl.ds(pl.multiple_of((x * C + c) * TOK, TOK), TOK), :]
    for chunk in range(COLS // CHUNK):
        send(chunk, CHUNK).wait()
    send(COLS // CHUNK, LOSS_LANES).wait()


def add_core(own_ref, other_ref, mine_ref, one_ref, two_ref, three_ref):
    here = lax.axis_index("x")
    for shift, ref in enumerate((mine_ref, one_ref, two_ref, three_ref)):
        x = lax.rem(here + shift, X)
        ref[...] = (own_ref[x] + other_ref[x]).astype(ref.dtype)


def add_x(mine_ref, one_ref, two_ref, three_ref, out_ref):
    total = mine_ref[...] + one_ref[...].astype(f32) + two_ref[...].astype(f32) + three_ref[...].astype(f32)
    out_ref[...] = total.astype(bf16)


def scatter_rows(pos_ref, rows_ref, own_ref, one_ref, two_ref, three_ref, out_ref, all_ref):
    y = lax.axis_index("y")
    for shift, ref in enumerate((own_ref, one_ref, two_ref, three_ref)):
        all_ref[lax.rem(y - shift + Y, Y)] = ref[...].astype(f32)
    grad_unit = all_ref[0]
    for other in range(1, Y):
        grad_unit = grad_unit + all_ref[other]
    grad_unit = grad_unit * student_scale
    rows = rows_ref[...]
    row_inv = unit_inverse(rows)
    along = jnp.sum(rows * grad_unit, axis=1, keepdims=True)
    grad_rows = row_inv * grad_unit - rows * (row_inv * row_inv * row_inv) * along
    where = lax.broadcasted_iota(jnp.int32, (FEAT, TOK), 0) == pos_ref[...]
    picker = jnp.where(where, 1.0, 0.0).astype(bf16)
    high, _ = split(grad_rows)
    mid, low = split(grad_rows - high.astype(f32))
    out_ref[...] = (
        jnp.dot(picker, high, preferred_element_type=f32)
        + jnp.dot(picker, mid, preferred_element_type=f32)
        + jnp.dot(picker, low, preferred_element_type=f32)
    )


def add_groups(core, recv_ref, out_ref):
    first = core == 0
    for x in range(X):
        for chunk in range(COLS // CHUNK):
            cols = pl.ds(chunk * CHUNK, CHUNK)
            total = recv_ref[x, :, cols].astype(f32)
            for z in range(1, Z):
                total = total + recv_ref[z * X + x, :, cols].astype(f32)
            there = pl.ds(x * COLS + chunk * CHUNK, CHUNK)
            out_ref[:, there] = jnp.where(first, total[0:4], total[4:8])


def add_theirs(recv_ref, out_ref):
    add_groups(1 - lax.axis_index("c"), recv_ref, out_ref)


def add_mine(recv_ref, out_ref, loss_ref):
    add_groups(lax.axis_index("c"), recv_ref, out_ref)
    loss = recv_ref[0, :, COLS : COLS + LANE].astype(f32)
    for z in range(1, Z):
        loss = loss + recv_ref[z * X, :, COLS : COLS + LANE].astype(f32)
    lane = lax.broadcasted_iota(jnp.int32, loss.shape, 1)
    loss_ref[...] = jnp.sum(jnp.where(lane < 3, loss, 0.0)[0:1, :], axis=1, keepdims=True)


def join(own_ref, other_ref, out_ref):
    core = lax.axis_index("c")
    for x in range(X):
        for ref, c in ((own_ref, core), (other_ref, 1 - core)):
            there = pl.ds(pl.multiple_of((x * C + c) * COLS, COLS), COLS)
            out_ref[:, there] = ref[:, x * COLS : (x + 1) * COLS]


def exchange(message, axes):
    return lax.all_to_all(message, axes, 0, 0)


def other_core(values):
    return lax.ppermute(values, "c", [(0, 1), (1, 0)])


def shifted(values, axis, size, shift):
    return lax.ppermute(values, axis, [(i, (i + shift) % size) for i in range(size)])


def local(teacher_seq, student_seq, prototypes, positions, languages):
    shape = jax.ShapeDtypeStruct
    kept = pltpu.VMEM
    sems = pltpu.SemaphoreType.DMA
    z_axis, row_axes = ("z",), ("x", "c", "y")
    pos = positions[None, :]

    units, rows = call(
        pick_rows,
        (shape((X, TOK + 16, 2 * FEAT), bf16), shape((TOK, FEAT), f32)),
        [
            pltpu.VMEM((1, TOK), jnp.int32),
            pltpu.VMEM((1, TOK), jnp.int32),
            pltpu.VMEM((FEAT, FEAT), bf16),
            pltpu.VMEM((FEAT, FEAT), bf16),
            sems((4,)),
        ],
        anywhere=(0, 1, 2, 3),
    )(pos, languages[None, :], teacher_seq, student_seq)
    w, unit, inv = call(
        weights,
        (shape((FEAT, COLS), bf16), shape((FEAT, COLS), bf16), shape((1, COLS), f32)),
        [sems((1,))],
        anywhere=(0,),
    )(prototypes)
    totals = pltpu.VMEM((ROWS, LANE), f32)
    products = pltpu.VMEM((ROWS, CHUNK), f32)
    small = shape((8, LANE), f32)
    units = exchange(units, ("x",))
    e, logits, turned, lang, count, message, rest = call(
        start,
        (
            kept((ROWS, COLS), f32),
            kept((ROWS, COLS), f32),
            shape((FEAT, ROWS), bf16),
            shape((8, LANE), f32),
            shape((8, LANE), f32),
            shape((PEERS, 16, LANE), bf16),
            small,
        ),
        [pltpu.VMEM((ROWS, FEAT), bf16), pltpu.VMEM((ROWS, FEAT), bf16), totals, totals, products],
    )(units, other_core(units), unit)

    arrived = []
    for sweep in range(ITERS):
        arrived.append(exchange(message, row_axes))
        out = shape((Z, 32 if sweep == 0 else 16, LANE), bf16 if sweep < ITERS - 1 else f32)
        message = call(column_pass, out, [pltpu.VMEM((COLS // LANE, 8, LANE), f32)])(arrived[-1], e, count)
        columns = exchange(message, z_axis)
        if sweep == 0:
            message, counts = call(row_first, (shape((PEERS, 16, LANE), bf16), small))(columns, e, rest)
        elif sweep < ITERS - 1:
            message = call(row_pass, shape((PEERS, 8, LANE), f32))(columns, e)
        else:
            message, col = call(row_last, (shape((PEERS, 16, LANE), f32), shape((16, LANE), f32)))(columns, e, logits)
    last = exchange(message, row_axes)
    grad, own, send = call(
        gradients,
        (pltpu.HBM((FEAT, COLS + LOSS_LANES), bf16), shape((X, TOK, FEAT), f32), shape((X, TOK, FEAT), f32)),
        [
            totals,
            totals,
            pltpu.VMEM((ROWS, COLS), bf16),
            pltpu.VMEM((FEAT, COLS + LOSS_LANES), bf16),
            pltpu.VMEM((ROWS, FEAT), f32),
            sems((COLS // CHUNK + 1,)),
        ],
        out_anywhere=(0,),
    )(last, arrived[0], arrived[1], lang, counts, e, logits, col, turned, unit, w, inv)
    block = shape((TOK, FEAT), f32)
    short = shape((TOK, FEAT), bf16)
    mine, *parts = call(add_core, (block, short, short, short))(own, other_core(send))
    mine = call(add_x, short)(mine, *(shifted(part, "x", X, s) for s, part in enumerate(parts, 1)))
    others = [shifted(mine, "y", Y, s) for s in range(1, Y)]
    grad = exchange(grad.reshape(Z * X, 8, COLS + LOSS_LANES), ("z", "x"))
    grad_student = call(
        scatter_rows,
        shape((FEAT, FEAT), f32),
        [pltpu.VMEM((Y, TOK, FEAT), f32)],
    )(pos, rows, mine, *others)
    grad, grad_student = lax.optimization_barrier((grad, grad_student))
    half = shape((4, X * COLS), f32)
    theirs = other_core(call(add_theirs, half)(grad))
    mine, loss = call(add_mine, (half, shape((1, 1), f32)))(grad)
    grad_prototypes = call(join, shape((4, GROUPS * COLS), f32))(mine, theirs)
    return (loss[0, 0], grad_student, grad_prototypes)


def solution(mesh):
    fine = Mesh(mesh.devices.reshape(Z, X, C, Y), ("z", "x", "c", "y"))
    tok = ("z", "x", "c")
    in_specs = (P(tok, None), P(tok, None), P(None, "y"), P(tok), P(tok))
    out_specs = (P(), P(tok, None), P(tok, "y"))
    return jax.shard_map(local, mesh=fine, in_specs=in_specs, out_specs=out_specs, check_vma=False)
```

```python
import jax
import jax.numpy as jnp
from jax import lax
from jax.experimental import pallas as pl
from jax.experimental.pallas import tpu as pltpu
from jax.sharding import Mesh, PartitionSpec as P

LANGS = 100
ITERS = 3

epsilon = 1e-06
teacher_scale = 20.0
student_scale = 10.0
grad_scale = 8388608.0

Z, X, C, Y = 8, 4, 2, 4
TOK = 128
GROUPS = X * C
ROWS = GROUPS * TOK
COLS = 2048
FEAT = 256
LANE = 128
CHUNK = 512
PARTS = CHUNK // LANE
PEERS = X * C * Y
LOSS_LANES = 128
f32 = jnp.float32
bf16 = jnp.bfloat16


def call(kernel, out_shape, scratch=(), anywhere=(), out_anywhere=(), mib=24):
    def run(*args):
        space = lambda far: pl.BlockSpec(memory_space=pltpu.HBM if far else pltpu.VMEM)
        args = [pltpu.with_memory_space_constraint(a, pltpu.HBM) if i in anywhere else a for i, a in enumerate(args)]
        multiple = isinstance(out_shape, (tuple, list))
        outs = [space(i in out_anywhere) for i in range(len(out_shape) if multiple else 1)]
        return pl.pallas_call(
            kernel,
            out_shape=out_shape,
            in_specs=[space(i in anywhere) for i in range(len(args))],
            out_specs=outs if multiple else outs[0],
            scratch_shapes=list(scratch),
            compiler_params=pltpu.CompilerParams(vmem_limit_bytes=mib << 20),
            name=kernel.__name__,
        )(*args)

    return run


def lanes(row):
    return jnp.broadcast_to(row, (LANE, LANE)).T


def row_totals(block):
    return jnp.sum(block.T, axis=0, keepdims=True)


def blk(index):
    return pl.ds(index * LANE, LANE)


def split(values):
    high = values.astype(bf16)
    return high, (values - high.astype(f32)).astype(bf16)


def nt(left, right):
    return lax.dot_general(left, right, (((1,), (1,)), ((), ())), preferred_element_type=f32)


def tn(left, right):
    return lax.dot_general(left, right, (((0,), (0,)), ((), ())), preferred_element_type=f32)


def unit_inverse(values):
    return lax.rsqrt(jnp.sum(values * values, axis=1, keepdims=True) + epsilon)


def fetch(sources, targets, sems):
    copies = [pltpu.make_async_copy(a, b, sems.at[n]) for n, (a, b) in enumerate(zip(sources, targets))]
    for copy in copies:
        copy.start()
    for copy in copies:
        copy.wait()


def pick_rows(pos_hbm, lang_hbm, teacher_hbm, student_hbm, out_ref, rows_ref, pos_ref, lang_ref, teacher_ref, student_ref, sems):
    fetch((pos_hbm, lang_hbm, teacher_hbm, student_hbm), (pos_ref, lang_ref, teacher_ref, student_ref), sems)
    where = lax.broadcasted_iota(jnp.int32, (FEAT, TOK), 0) == pos_ref[...]
    picker = jnp.where(where, 1.0, 0.0).astype(bf16)
    teacher = tn(picker, teacher_ref[...])
    student = tn(picker, student_ref[...])
    teacher_unit = (teacher * unit_inverse(teacher)).astype(bf16)
    student_unit = (student * unit_inverse(student)).astype(bf16)
    language = jnp.broadcast_to(lang_ref[...].astype(f32), (16, TOK)).astype(bf16)
    rows_ref[...] = student
    for peer in range(X):
        out_ref[peer, 0:TOK, 0:FEAT] = teacher_unit
        out_ref[peer, 0:TOK, FEAT : 2 * FEAT] = student_unit
        for part in range(4):
            out_ref[peer, TOK : TOK + 16, part * LANE : (part + 1) * LANE] = language


def weights(proto_hbm, w_ref, unit_ref, inv_ref, sems):
    group = lax.axis_index("x") * C + lax.axis_index("c")
    here = pl.ds(pl.multiple_of(group * COLS, COLS), COLS)
    fetch((proto_hbm.at[:, here],), (w_ref,), sems)
    for chunk in range(COLS // CHUNK):
        cols = pl.ds(chunk * CHUNK, CHUNK)
        w = w_ref[:, cols].astype(f32)
        inv = lax.rsqrt(jnp.sum(w * w, axis=0, keepdims=True) + epsilon)
        inv_ref[:, cols] = inv
        unit_ref[:, cols] = (w * inv).astype(bf16)


def lane_sum(block):
    total = block[:, 0:LANE]
    for part in range(1, PARTS):
        total = total + block[:, part * LANE : (part + 1) * LANE]
    return total


def all_row_totals(acc_ref):
    return jnp.concatenate([row_totals(acc_ref[blk(k), :]) for k in range(GROUPS)], axis=0)


HALF = X


def pick(refs, k):
    return refs[k // HALF].at[blk(k % HALF), :]


def swap(values):
    return jnp.where(lax.axis_index("c") == 0, values, jnp.concatenate([values[HALF:], values[:HALF]], axis=0))


def start_half(recv_ref, unit_ref, e_ref, logit_ref, turned_ref, lang_ref, stat_ref, teacher_ref, student_ref, acc_ref, exp_ref, d_ref):
    for x in range(X):
        teacher_ref[blk(x), :] = recv_ref[x, 0:TOK, 0:FEAT]
        student_ref[blk(x), :] = recv_ref[x, 0:TOK, FEAT : 2 * FEAT]
        lang_ref[x : x + 1, :] = recv_ref[x, TOK : TOK + 16, 0:LANE].astype(f32)[0:1, :]
        turned_ref[:, blk(x)] = student_ref[blk(x), :].astype(f32).T.astype(bf16)
    acc_ref[...] = jnp.zeros((HALF * TOK, LANE), f32)
    exp_ref[...] = jnp.zeros((HALF * TOK, LANE), f32)
    for chunk in range(COLS // CHUNK):
        cols = pl.ds(chunk * CHUNK, CHUNK)
        unit = unit_ref[:, cols]
        d_ref[...] = jnp.dot(teacher_ref[...], unit, preferred_element_type=f32)
        logit_ref[:, cols] = jnp.dot(student_ref[...], unit, preferred_element_type=f32)
        for k in range(HALF):
            e = jnp.exp(d_ref[blk(k), :] * teacher_scale)
            e_ref[blk(k), cols] = e
            acc_ref[blk(k), :] += lane_sum(e)
            exp_ref[blk(k), :] += lane_sum(jnp.exp(logit_ref[blk(k), cols] * student_scale))
    stat_ref[...] = jnp.concatenate(
        [row_totals(acc_ref[blk(k), :]) for k in range(HALF)] + [row_totals(exp_ref[blk(k), :]) for k in range(HALF)], axis=0
    )


def start_own(*refs):
    start_half(*refs)


def start_other(
    recv_ref, unit_ref, own_turned_ref, own_lang_ref, own_stat_ref,
    e_ref, logit_ref, turned_ref, lang_ref, count_ref, msg_ref, rest_ref,
    half_turned_ref, half_lang_ref, stat_ref, *work,
):
    start_half(recv_ref, unit_ref, e_ref, logit_ref, half_turned_ref, half_lang_ref, stat_ref, *work)
    turned_ref[:, 0 : HALF * TOK] = own_turned_ref[...]
    turned_ref[:, HALF * TOK : ROWS] = half_turned_ref[...]
    lang_ref[0:HALF, :] = own_lang_ref[...]
    lang_ref[HALF : 2 * HALF, :] = half_lang_ref[...]
    hits = jnp.zeros((LANE, LANE), f32)
    number = lax.broadcasted_iota(jnp.int32, (LANE, LANE), 0).astype(f32)
    for k in range(GROUPS):
        hits = hits + jnp.where(number == lang_ref[k : k + 1, :], 1.0, 0.0)
    count_ref[...] = jnp.broadcast_to(row_totals(hits), (8, LANE))
    own, other = own_stat_ref[...], stat_ref[...]
    sums = swap(jnp.concatenate([own[:HALF], other[:HALF]], axis=0))
    high, rest = split(swap(jnp.concatenate([own[HALF:], other[HALF:]], axis=0)))
    rest_ref[...] = rest.astype(f32)
    send_pair(msg_ref, sums, high.astype(f32))


def send_rows(msg_ref, *parts):
    for peer in range(PEERS):
        for n, part in enumerate(parts):
            msg_ref[peer, 8 * n : 8 * n + 8, :] = part


def two_parts(values):
    high, low = split(values)
    return jnp.concatenate([high.astype(f32), low.astype(f32)], axis=0).astype(bf16)


def send_pair(msg_ref, first, second):
    both = jnp.concatenate([first, second], axis=0).astype(bf16)
    for peer in range(PEERS):
        msg_ref[peer] = both


def peer_sum(recv_ref, low, high):
    total = recv_ref[0, low:high, :].astype(f32)
    for peer in range(1, recv_ref.shape[0]):
        total = total + recv_ref[peer, low:high, :].astype(f32)
    return total


def column_pass(recv_ref, own_ref, other_ref, count_ref, msg_ref, acc_ref):
    rows = 16 if recv_ref.dtype == bf16 else 8
    row_weight = swap(1.0 / peer_sum(recv_ref, 0, rows)[0:8])
    for k in range(GROUPS):
        factor = lanes(row_weight[k : k + 1, :])
        for j in range(COLS // LANE):
            part = jnp.sum((pick((own_ref, other_ref), k)[:, blk(j)] * factor).reshape(LANE // 8, 8, LANE), axis=0)
            acc_ref[j] = part if k == 0 else acc_ref[j] + part
    sums = jnp.concatenate([jnp.sum(acc_ref[j], axis=0, keepdims=True) for j in range(COLS // LANE)], axis=0)
    counts = two_parts(count_ref[...])
    for peer in range(Z):
        msg_ref[peer, 0:16, :] = sums.astype(msg_ref.dtype)
        if msg_ref.shape[1] > 16:
            msg_ref[peer, 16:32, :] = counts


def weighted_rows(e_refs, col_weight):
    out = []
    for k in range(GROUPS):
        e_ref = pick(e_refs, k)
        acc = e_ref[:, blk(0)] * col_weight[0:1, :]
        for j in range(1, COLS // LANE):
            acc = acc + e_ref[:, blk(j)] * col_weight[j : j + 1, :]
        out.append(row_totals(acc))
    return swap(jnp.concatenate(out, axis=0))


def row_first(recv_ref, own_ref, other_ref, rest_ref, msg_ref, count_ref):
    counts = peer_sum(recv_ref, 16, 32)
    count_ref[...] = counts[0:8] + counts[8:16]
    send_pair(msg_ref, weighted_rows((own_ref, other_ref), 1.0 / peer_sum(recv_ref, 0, 16)), rest_ref[...])


def row_pass(recv_ref, own_ref, other_ref, msg_ref):
    send_rows(msg_ref, weighted_rows((own_ref, other_ref), 1.0 / peer_sum(recv_ref, 0, 16)))


def row_last(recv_ref, own_ref, other_ref, own_logit_ref, other_logit_ref, msg_ref, col_ref):
    col_weight = 1.0 / peer_sum(recv_ref, 0, 16)
    col_ref[...] = col_weight
    sums, dots = [], []
    for k in range(GROUPS):
        e_ref, logit_ref = pick((own_ref, other_ref), k), pick((own_logit_ref, other_logit_ref), k)
        total = e_ref[:, blk(0)] * col_weight[0:1, :]
        dot = total * logit_ref[:, blk(0)]
        for j in range(1, COLS // LANE):
            t = e_ref[:, blk(j)] * col_weight[j : j + 1, :]
            total = total + t
            dot = dot + t * logit_ref[:, blk(j)]
        sums.append(row_totals(total))
        dots.append(row_totals(dot) * student_scale)
    send_rows(msg_ref, swap(jnp.concatenate(sums, axis=0)), swap(jnp.concatenate(dots, axis=0)))


def gradients(
    last_ref, first_ref, second_ref, lang_ref, count_ref, own_e_ref, other_e_ref, own_logit_ref, other_logit_ref, col_ref, turned_ref, unit_ref, w_ref, inv_ref,
    out_hbm, own_ref, send_ref, a_ref, b_ref, g_ref, out_ref, u_ref, sems,
):
    row_sum = swap(peer_sum(last_ref, 0, 8))
    dot_sum = swap(peer_sum(last_ref, 8, 16))
    exp_sum = swap(peer_sum(first_ref, 0, 16)[8:16] + peer_sum(second_ref, 0, 16)[8:16])
    row_weight = 1.0 / row_sum
    target_sum = row_weight * row_sum
    cross = jnp.log(exp_sum) * target_sum - row_weight * dot_sum

    counts = count_ref[0:1, :]
    present = jnp.sum(jnp.where(counts > 0.5, 1.0, 0.0), axis=1, keepdims=True)
    count_rows = lanes(counts)
    number = lax.broadcasted_iota(jnp.int32, (LANE, LANE), 0).astype(f32)
    own = [
        jnp.sum(jnp.where(number == lang_ref[k : k + 1, :], count_rows, 0.0), axis=0, keepdims=True)
        for k in range(GROUPS)
    ]
    token_weight = 1.0 / (jnp.concatenate(own, axis=0) * present)
    loss = jnp.sum(jnp.sum(token_weight * cross, axis=1, keepdims=True), axis=0, keepdims=True)
    soft_factor = grad_scale * token_weight * target_sum / exp_sum
    target_factor = grad_scale * token_weight * row_weight
    for k in range(GROUPS):
        a_ref[blk(k), :] = lanes(soft_factor[k : k + 1, :])
        b_ref[blk(k), :] = lanes(target_factor[k : k + 1, :])

    def send(chunk, width):
        cols = pl.ds(pl.multiple_of(chunk * CHUNK, CHUNK), width)
        return pltpu.make_async_copy(out_ref.at[:, cols], out_hbm.at[:, cols], sems.at[chunk])

    loss_high, _ = split(loss)
    loss_mid, loss_low = split(loss - loss_high.astype(f32))
    lane = lax.broadcasted_iota(jnp.int32, (FEAT, LANE), 1)
    packed = jnp.where(lane == 0, loss_high.astype(f32), jnp.where(lane == 1, loss_mid.astype(f32), loss_low.astype(f32)))
    out_ref[:, COLS : COLS + LANE] = packed.astype(bf16)
    send(COLS // CHUNK, LOSS_LANES).start()

    for chunk in range(COLS // CHUNK):
        cols = pl.ds(chunk * CHUNK, CHUNK)
        for k in range(GROUPS):
            a, b = a_ref[blk(k), :], b_ref[blk(k), :]
            e_ref, logit_ref = pick((own_e_ref, other_e_ref), k), pick((own_logit_ref, other_logit_ref), k)
            for part in range(PARTS):
                j = chunk * PARTS + part
                soft = a * jnp.exp(logit_ref[:, blk(j)] * student_scale)
                target = b * e_ref[:, blk(j)] * col_ref[j : j + 1, :]
                g_ref[blk(k), blk(j)] = (soft - target).astype(bf16)
        full = jnp.dot(turned_ref[...], g_ref[:, cols], preferred_element_type=f32) * student_scale
        w = w_ref[:, cols].astype(f32)
        inv = inv_ref[:, cols]
        inner = jnp.sum(w * full, axis=0, keepdims=True)
        out_ref[:, cols] = (inv * full - w * (inv * inv * inv * inner)).astype(bf16)
        send(chunk, CHUNK).start()
    u_ref[...] = nt(g_ref[...], unit_ref[...])
    for x in range(X):
        own_ref[x] = u_ref[blk(x), :]
        send_ref[x] = u_ref[blk(HALF + x), :]
    for chunk in range(COLS // CHUNK):
        send(chunk, CHUNK).wait()
    send(COLS // CHUNK, LOSS_LANES).wait()


def add_core(own_ref, other_ref, mine_ref, one_ref, two_ref, three_ref):
    here = lax.axis_index("x")
    for shift, ref in enumerate((mine_ref, one_ref, two_ref, three_ref)):
        x = lax.rem(here + shift, X)
        ref[...] = (own_ref[x] + other_ref[x]).astype(ref.dtype)


def add_x(mine_ref, one_ref, two_ref, three_ref, out_ref):
    total = mine_ref[...] + one_ref[...].astype(f32) + two_ref[...].astype(f32) + three_ref[...].astype(f32)
    out_ref[...] = total.astype(bf16)


def scatter_rows(pos_ref, rows_ref, own_ref, one_ref, two_ref, three_ref, out_ref, all_ref):
    y = lax.axis_index("y")
    for shift, ref in enumerate((own_ref, one_ref, two_ref, three_ref)):
        all_ref[lax.rem(y - shift + Y, Y)] = ref[...].astype(f32)
    grad_unit = all_ref[0]
    for other in range(1, Y):
        grad_unit = grad_unit + all_ref[other]
    grad_unit = grad_unit * student_scale
    rows = rows_ref[...]
    row_inv = unit_inverse(rows)
    along = jnp.sum(rows * grad_unit, axis=1, keepdims=True)
    grad_rows = row_inv * grad_unit - rows * (row_inv * row_inv * row_inv) * along
    where = lax.broadcasted_iota(jnp.int32, (FEAT, TOK), 0) == pos_ref[...]
    picker = jnp.where(where, 1.0, 0.0).astype(bf16)
    high, _ = split(grad_rows)
    mid, low = split(grad_rows - high.astype(f32))
    out_ref[...] = (
        jnp.dot(picker, high, preferred_element_type=f32)
        + jnp.dot(picker, mid, preferred_element_type=f32)
        + jnp.dot(picker, low, preferred_element_type=f32)
    )


def add_groups(core, recv_ref, out_ref):
    first = core == 0
    for x in range(X):
        for chunk in range(COLS // CHUNK):
            cols = pl.ds(chunk * CHUNK, CHUNK)
            total = recv_ref[x, :, cols].astype(f32)
            for z in range(1, Z):
                total = total + recv_ref[z * X + x, :, cols].astype(f32)
            there = pl.ds(x * COLS + chunk * CHUNK, CHUNK)
            out_ref[:, there] = jnp.where(first, total[0:4], total[4:8])


def add_theirs(recv_ref, out_ref):
    add_groups(1 - lax.axis_index("c"), recv_ref, out_ref)


def add_mine(recv_ref, out_ref, loss_ref):
    add_groups(lax.axis_index("c"), recv_ref, out_ref)
    loss = recv_ref[0, :, COLS : COLS + LANE].astype(f32)
    for z in range(1, Z):
        loss = loss + recv_ref[z * X, :, COLS : COLS + LANE].astype(f32)
    lane = lax.broadcasted_iota(jnp.int32, loss.shape, 1)
    loss_ref[...] = jnp.sum(jnp.where(lane < 3, loss, 0.0)[0:1, :], axis=1, keepdims=True)


def join(own_ref, other_ref, out_ref):
    core = lax.axis_index("c")
    for x in range(X):
        for ref, c in ((own_ref, core), (other_ref, 1 - core)):
            there = pl.ds(pl.multiple_of((x * C + c) * COLS, COLS), COLS)
            out_ref[:, there] = ref[:, x * COLS : (x + 1) * COLS]


def exchange(message, axes):
    return lax.all_to_all(message, axes, 0, 0)


def other_core(values):
    return lax.ppermute(values, "c", [(0, 1), (1, 0)])


def shifted(values, axis, size, shift):
    return lax.ppermute(values, axis, [(i, (i + shift) % size) for i in range(size)])


def local(teacher_seq, student_seq, prototypes, positions, languages):
    shape = jax.ShapeDtypeStruct
    kept = pltpu.VMEM
    sems = pltpu.SemaphoreType.DMA
    z_axis, row_axes = ("z",), ("x", "c", "y")
    pos = positions[None, :]

    units, rows = call(
        pick_rows,
        (shape((X, TOK + 16, 2 * FEAT), bf16), shape((TOK, FEAT), f32)),
        [
            pltpu.VMEM((1, TOK), jnp.int32),
            pltpu.VMEM((1, TOK), jnp.int32),
            pltpu.VMEM((FEAT, FEAT), bf16),
            pltpu.VMEM((FEAT, FEAT), bf16),
            sems((4,)),
        ],
        anywhere=(0, 1, 2, 3),
    )(pos, languages[None, :], teacher_seq, student_seq)
    w, unit, inv = call(
        weights,
        (shape((FEAT, COLS), bf16), shape((FEAT, COLS), bf16), shape((1, COLS), f32)),
        [sems((1,))],
        anywhere=(0,),
    )(prototypes)
    totals = pltpu.VMEM((ROWS, LANE), f32)
    small = shape((8, LANE), f32)
    units, w, unit, inv = lax.optimization_barrier((exchange(units, ("x",)), w, unit, inv))
    rest_units = other_core(units)
    held = kept((HALF * TOK, COLS), f32)
    short = shape((HALF, LANE), f32)
    half_turned = shape((FEAT, HALF * TOK), bf16)
    work = [
        pltpu.VMEM((HALF * TOK, FEAT), bf16),
        pltpu.VMEM((HALF * TOK, FEAT), bf16),
        pltpu.VMEM((HALF * TOK, LANE), f32),
        pltpu.VMEM((HALF * TOK, LANE), f32),
        pltpu.VMEM((HALF * TOK, CHUNK), f32),
    ]
    own_e, own_logits, own_turned, own_lang, own_stat = call(start_own, (held, held, half_turned, short, small), work)(
        units, unit
    )
    other_e, other_logits, turned, lang, count, message, rest = call(
        start_other,
        (held, held, shape((FEAT, ROWS), bf16), small, small, shape((PEERS, 16, LANE), bf16), small),
        [pltpu.VMEM((FEAT, HALF * TOK), bf16), pltpu.VMEM((HALF, LANE), f32), pltpu.VMEM((8, LANE), f32)] + work,
    )(rest_units, unit, own_turned, own_lang, own_stat)
    e = (own_e, other_e)
    logits = (own_logits, other_logits)

    arrived = []
    for sweep in range(ITERS):
        arrived.append(exchange(message, row_axes))
        out = shape((Z, 32 if sweep == 0 else 16, LANE), bf16 if sweep < ITERS - 1 else f32)
        message = call(column_pass, out, [pltpu.VMEM((COLS // LANE, 8, LANE), f32)])(arrived[-1], *e, count)
        columns = exchange(message, z_axis)
        if sweep == 0:
            message, counts = call(row_first, (shape((PEERS, 16, LANE), bf16), small))(columns, *e, rest)
        elif sweep < ITERS - 1:
            message = call(row_pass, shape((PEERS, 8, LANE), f32))(columns, *e)
        else:
            message, col = call(row_last, (shape((PEERS, 16, LANE), f32), shape((16, LANE), f32)))(columns, *e, *logits)
    last = exchange(message, row_axes)
    grad, own, send = call(
        gradients,
        (pltpu.HBM((FEAT, COLS + LOSS_LANES), bf16), shape((X, TOK, FEAT), f32), shape((X, TOK, FEAT), f32)),
        [
            totals,
            totals,
            pltpu.VMEM((ROWS, COLS), bf16),
            pltpu.VMEM((FEAT, COLS + LOSS_LANES), bf16),
            pltpu.VMEM((ROWS, FEAT), f32),
            sems((COLS // CHUNK + 1,)),
        ],
        out_anywhere=(0,),
    )(last, arrived[0], arrived[1], lang, counts, *e, *logits, col, turned, unit, w, inv)
    block = shape((TOK, FEAT), f32)
    short = shape((TOK, FEAT), bf16)
    mine, *parts = call(add_core, (block, short, short, short))(own, other_core(send))
    mine = call(add_x, short)(mine, *(shifted(part, "x", X, s) for s, part in enumerate(parts, 1)))
    others = [shifted(mine, "y", Y, s) for s in range(1, Y)]
    grad = exchange(grad.reshape(Z * X, 8, COLS + LOSS_LANES), ("z", "x"))
    grad_student = call(
        scatter_rows,
        shape((FEAT, FEAT), f32),
        [pltpu.VMEM((Y, TOK, FEAT), f32)],
    )(pos, rows, mine, *others)
    grad, grad_student = lax.optimization_barrier((grad, grad_student))
    half = shape((4, X * COLS), f32)
    theirs = other_core(call(add_theirs, half)(grad))
    mine, loss = call(add_mine, (half, shape((1, 1), f32)))(grad)
    grad_prototypes = call(join, shape((4, GROUPS * COLS), f32))(mine, theirs)
    return (loss[0, 0], grad_student, grad_prototypes)


def solution(mesh):
    fine = Mesh(mesh.devices.reshape(Z, X, C, Y), ("z", "x", "c", "y"))
    tok = ("z", "x", "c")
    in_specs = (P(tok, None), P(tok, None), P(None, "y"), P(tok), P(tok))
    out_specs = (P(), P(tok, None), P(tok, "y"))
    return jax.shard_map(local, mesh=fine, in_specs=in_specs, out_specs=out_specs, check_vma=False)
```
